512 devices in a mesh: ta: 16 (over y, core), gz: 8 (over z), gy: 4 (over x).
Axes of the slice: x: 4, y: 8, z: 8, core: 2. Of those that a mesh axis runs over, the one named last changes fastest.
Arguments:
- restricted: bfloat16 [4096, 2, 64, 256], P(('ta', 'gz', 'gy')), may hold values from -30 to 30
- couplings: bfloat16 [9, 1, 8, 16, 32, 64, 128], P(None, None, 'gy', 'gz', 'ta'), may hold values from -3 to 7
- owners: int32 [4096], P(('ta', 'gz', 'gy')), may hold values from 0 to 7, as said below
- coarse_site: int32 [4096], P(('ta', 'gz', 'gy')), may hold values from 0 to 7, as said below
Outputs:
- solution: bfloat16 [1, 8, 16, 32, 2, 64, 256], P(None, 'gy', 'gz', 'ta')
The draws below stay inside these ranges and needn't reach their ends.
Inputs may be any that keep to these rules, and one draw needn't show every extreme that they name: `owners`: within one ta and gy index, every device sends exactly 1 of its aggregates to each device of its gz group. Within one ta and gy index, the pairs (owners, coarse_site) are all different: every coarse site receives exactly one aggregate.
All inputs are finite; a program needn't handle non-finite values.
Results may differ from the reference program's by a relative error of at most 0.0065.
Values may be sent and summed in bfloat16 or wider, within the bound.
No kernel may reach another device: no remote copies, remote signals or barrier semaphores. Data moves between devices by JAX's collectives and lax.ppermute only.
A program may use at most 128 MiB of HBM per device.

```python
import jax
import jax.numpy as jnp
from jax import lax

DOF = 64
RHS = 256
LY = 2
LZ = 2
LT = 2
AGG_DEV = 8
BUCKET = 1
AGG_ROWS = 4096
CX = 1
CY = 8
CZ = 16
CT = 32
N_TA = 16
N_GZ = 8
N_GY = 4


def pairing(key):
    shape = (N_TA, N_GZ, N_GY, AGG_DEV)
    tiebreak = jnp.arange(AGG_DEV, dtype=jnp.int32)
    sender_keys = jax.random.randint(jax.random.fold_in(key, 101), shape, 0, 1 << 20) * AGG_DEV + tiebreak
    sigma = jnp.argsort(sender_keys, axis=-1, stable=True).astype(jnp.int32)
    receiver_keys = jax.random.randint(jax.random.fold_in(key, 202), shape, 0, 1 << 20) * AGG_DEV + tiebreak
    tau = jnp.argsort(receiver_keys, axis=-1, stable=True).astype(jnp.int32)
    owner_grid = sigma // BUCKET
    along_t = jnp.arange(N_TA, dtype=jnp.int32)[:, None, None, None]
    along_z = jnp.arange(N_GZ, dtype=jnp.int32)[None, :, None, None]
    along_y = jnp.arange(N_GY, dtype=jnp.int32)[None, None, :, None]
    incoming = along_z * BUCKET + sigma % BUCKET
    site_grid = tau[along_t, owner_grid, along_y, incoming]
    return (owner_grid.reshape(AGG_ROWS), site_grid.reshape(AGG_ROWS))


def draw_owners(key, part):
    return pairing(key)[0]


def draw_coarse_site(key, part):
    return pairing(key)[1]


def draw_restricted(key, part):
    key = jax.random.fold_in(key, 13)
    first, second = jax.random.split(key, 2)
    shape = (AGG_ROWS, 2, DOF, RHS)
    device = (jnp.arange(AGG_ROWS) // AGG_DEV).astype(jnp.float32)
    ramp = 0.6 + 1.2 * device / max(AGG_ROWS // AGG_DEV - 1, 1)
    base = jnp.clip(jax.random.normal(first, shape, jnp.float32), -4.0, 4.0)
    row_scale = jnp.exp(jax.random.uniform(second, (AGG_ROWS,), jnp.float32, jnp.log(0.3), jnp.log(3.0)))
    scaled = base * (row_scale * ramp)[:, None, None, None]
    return scaled.astype(jnp.bfloat16)


def draw_couplings(key, part):
    key = jax.random.fold_in(key, 7)
    shape = (9, CX, CY, CZ, CT, DOF, 2 * DOF)
    time_pos = jnp.arange(CT, dtype=jnp.float32)[None, None, None, None, :, None, None]
    fraction = time_pos / max(CT - 1, 1)
    noise = jnp.clip(jax.random.normal(key, shape, jnp.float32), -4.0, 4.0)
    level = 1.5 * jnp.exp(fraction * jnp.log(3.0))
    direction = jnp.arange(9)[:, None, None, None, None, None, None]
    row_pos = jnp.arange(DOF)[None, None, None, None, None, :, None]
    col_pos = jnp.arange(2 * DOF)[None, None, None, None, None, None, :]
    scale = jnp.where(direction == 0, 0.03, 0.025)
    diagonal = jnp.where((direction == 0) & (row_pos == col_pos), level, 0.0)
    return (diagonal + scale * noise).astype(jnp.bfloat16)


def setup_inputs(seed: int = 0) -> dict:
    seeds = jax.random.split(jax.random.key(seed), 5)
    return {
        "restricted": draw_restricted(jax.random.fold_in(seeds[4], 71), 0),
        "couplings": draw_couplings(jax.random.fold_in(seeds[4], 71), 0),
        "owners": draw_owners(jax.random.fold_in(seeds[4], 71), 0),
        "coarse_site": draw_coarse_site(jax.random.fold_in(seeds[4], 71), 0),
    }


def block_double(blocks):
    columns = blocks.shape[-1] // 2
    real_blk = blocks[..., :columns]
    imag_blk = blocks[..., columns:]
    upper = jnp.concatenate([real_blk, -imag_blk], axis=-1)
    lower = jnp.concatenate([imag_blk, real_blk], axis=-1)
    return jnp.concatenate([upper, lower], axis=-2)


def slice_apply(blocks, values):
    shape = values.shape
    flat = values.reshape(shape[:-3] + (2 * shape[-2], shape[-1])).astype(jnp.float32)
    doubled = block_double(blocks.astype(jnp.float32))
    result = jnp.einsum("abcoi,abciw->abcow", doubled, flat, precision=lax.Precision.HIGHEST)
    return result.reshape(shape)


def operator(couplings, values):
    def one_slice(time_pos):
        current = lax.dynamic_index_in_dim(values, time_pos, 3, keepdims=False)
        ahead = lax.dynamic_index_in_dim(values, (time_pos + 1) % CT, 3, keepdims=False)
        behind = lax.dynamic_index_in_dim(values, (time_pos + CT - 1) % CT, 3, keepdims=False)
        blocks = lax.dynamic_index_in_dim(couplings, time_pos, 4, keepdims=False)
        neighbours = [jnp.roll(current, -1, 0), jnp.roll(current, 1, 0),
                      jnp.roll(current, -1, 1), jnp.roll(current, 1, 1),
                      jnp.roll(current, -1, 2), jnp.roll(current, 1, 2),
                      ahead, behind]
        result = slice_apply(blocks[0], current)
        for position in range(8):
            result = result + slice_apply(blocks[position + 1], neighbours[position])
        return result
    slices = lax.map(one_slice, jnp.arange(CT, dtype=jnp.int32))
    return jnp.moveaxis(slices, 0, 3)


def inner_product(first_vec, second_vec):
    keep = tuple(range(first_vec.ndim - 3)) + (first_vec.ndim - 3,)
    first_re = first_vec[..., 0, :, :]
    first_im = first_vec[..., 1, :, :]
    second_re = second_vec[..., 0, :, :]
    second_im = second_vec[..., 1, :, :]
    real_part = jnp.sum(first_re * second_re + first_im * second_im, axis=keep)
    imag_part = jnp.sum(first_re * second_im - first_im * second_re, axis=keep)
    return real_part, imag_part


def complex_scale(values, coef_re, coef_im):
    value_re = values[..., 0, :, :]
    value_im = values[..., 1, :, :]
    return jnp.stack([coef_re * value_re - coef_im * value_im, coef_re * value_im + coef_im * value_re], axis=-3)


def reference(restricted, couplings, owners, coarse_site):
    row_ids = jnp.arange(AGG_ROWS, dtype=jnp.int32)
    device = row_ids // AGG_DEV
    ta_index = device // (N_GZ * N_GY)
    gy_index = device % N_GY
    along_x = coarse_site // (LY * LZ * LT)
    along_y = gy_index * LY + (coarse_site // (LZ * LT)) % LY
    along_z = owners * LZ + (coarse_site // LT) % LZ
    along_t = ta_index * LT + coarse_site % LT
    source = jnp.zeros((CX, CY, CZ, CT, 2, DOF, RHS), jnp.bfloat16)
    source = source.at[along_x, along_y, along_z, along_t].set(restricted)
    start = source.astype(jnp.float32)
    image0 = operator(couplings, source)
    norm_zero = jnp.sum(image0 * image0, axis=tuple(range(image0.ndim - 1)))
    c_re, c_im = inner_product(image0, start)
    alpha_re = c_re / norm_zero
    alpha_im = c_im / norm_zero
    iterate = complex_scale(start, alpha_re, alpha_im)
    residual = start - complex_scale(image0, alpha_re, alpha_im)
    search = residual.astype(jnp.bfloat16)
    image1 = operator(couplings, search)
    proj_re, proj_im = inner_product(image0, image1)
    beta_re = proj_re / norm_zero
    beta_im = proj_im / norm_zero
    update = image1 - complex_scale(image0, beta_re, beta_im)
    direction = search.astype(jnp.float32) - complex_scale(start, beta_re, beta_im)
    num_re, num_im = inner_product(update, residual)
    denom = jnp.sum(update * update, axis=tuple(range(update.ndim - 1)))
    solution = iterate + complex_scale(direction, num_re / denom, num_im / denom)
    return solution.astype(jnp.bfloat16)
```

```python
import jax
import jax.numpy as jnp
from jax import lax
from jax.sharding import Mesh, PartitionSpec as P

ALL_AXES = ("ty", "tc", "gz", "gy")
TIME_AXES = ("ty", "tc")
SLOT_ROWS = 16


def axes_size(axes):
    return lax.axis_size(axes)


def shifted(values, axes, step):
    count = axes_size(axes)
    return lax.ppermute(values, axes, [(i, (i + step) % count) for i in range(count)])


def spread_sum(parts, axes):
    count = axes_size(axes)
    copies = jnp.broadcast_to(parts[None], (count,) + parts.shape)
    landed = lax.all_to_all(copies, axes, split_axis=0, concat_axis=0, tiled=True)
    return jnp.sum(landed, axis=0)


def block_double(blocks):
    columns = blocks.shape[-1] // 2
    real_blk = blocks[..., :columns]
    imag_blk = blocks[..., columns:]
    upper = jnp.concatenate([real_blk, -imag_blk], axis=-1)
    lower = jnp.concatenate([imag_blk, real_blk], axis=-1)
    return jnp.concatenate([upper, lower], axis=-2)


def relay(restricted, owners, coarse_site):
    count = restricted.shape[0]
    positions = jnp.arange(count, dtype=jnp.int32)
    picker = (owners[None, :] == positions[:, None]).astype(jnp.int32)
    order = jnp.sum(picker * positions[None, :], axis=1)
    rows = restricted.reshape(count, -1, restricted.shape[-1])
    tail = jnp.broadcast_to(
        coarse_site.astype(rows.dtype)[:, None, None], (count, SLOT_ROWS, rows.shape[-1])
    )
    payload = jnp.take(jnp.concatenate([rows, tail], axis=1), order, axis=0)
    landed = lax.all_to_all(payload, "gz", split_axis=0, concat_axis=0, tiled=True)
    slots = landed[:, rows.shape[1], 0].astype(jnp.int32)
    placer = (slots[None, :] == positions[:, None]).astype(jnp.int32)
    arrival = jnp.sum(placer * positions[None, :], axis=1)
    return jnp.take(landed[:, : rows.shape[1]], arrival, axis=0)


def exchange(field):
    outer = []
    for axes, dim in (("gz", 1), ("gy", 0), (TIME_AXES, 2)):
        head = lax.slice_in_dim(field, 0, 1, axis=dim)
        tail = lax.slice_in_dim(field, 1, 2, axis=dim)
        outer.append(
            jnp.concatenate([shifted(tail, axes, 1), shifted(head, axes, -1)], axis=dim)
        )
    return [outer[1], outer[0], outer[2]]


def split_couplings(doubled):
    inside = [doubled[0], doubled[1], doubled[2]]
    outside = []
    for dim in range(3):
        ahead, behind = doubled[3 + 2 * dim], doubled[4 + 2 * dim]
        pick = lambda a, s: lax.slice_in_dim(a, s, s + 1, axis=dim)
        inside.append(jnp.concatenate([pick(ahead, 0), pick(behind, 1)], axis=dim))
        outside.append(jnp.concatenate([pick(behind, 0), pick(ahead, 1)], axis=dim))
    return jnp.stack(inside), jnp.stack(outside)


def operate(inside, outside, field):
    outer = jnp.stack(exchange(field))
    inner = jnp.stack([field, field, field] + [jnp.flip(field, axis=d) for d in range(3)])
    form = "kabcoi,kabciw->abcow"
    near = jnp.einsum(form, inside, inner, preferred_element_type=jnp.float32)
    far = jnp.einsum(form, outside, outer, preferred_element_type=jnp.float32)
    return near + far


def dot_parts(first, second):
    half = first.shape[-2] // 2
    a_re, a_im = first[..., :half, :], first[..., half:, :]
    b_re, b_im = second[..., :half, :], second[..., half:, :]
    over = tuple(range(first.ndim - 1))
    real_part = jnp.sum(a_re * b_re + a_im * b_im, axis=over)
    imag_part = jnp.sum(a_re * b_im - a_im * b_re, axis=over)
    return real_part, imag_part


def local(restricted, couplings, owners, coarse_site):
    source = relay(restricted, owners, coarse_site).reshape((2, 2, 2, -1, restricted.shape[-1]))
    inside, outside = split_couplings(block_double(couplings[:, 0]))
    start = source.astype(jnp.float32)
    image = operate(inside, outside, source)
    second = operate(inside, outside, image.astype(jnp.bfloat16))
    over = tuple(range(image.ndim - 1))
    c_re, c_im = dot_parts(image, start)
    d_re, d_im = dot_parts(image, second)
    e_re, e_im = dot_parts(second, start)
    parts = jnp.stack(
        [
            jnp.sum(image * image, axis=over),
            c_re,
            c_im,
            d_re,
            d_im,
            e_re,
            e_im,
            jnp.sum(second * second, axis=over),
        ]
    )
    totals = spread_sum(spread_sum(parts, ("tc", "gz")), ("ty", "gy"))
    norm, c_re, c_im, d_re, d_im, e_re, e_im, tail = [totals[i] for i in range(8)]
    a_re, a_im = c_re / norm, c_im / norm
    g_re, g_im = d_re / norm, d_im / norm
    p_re, p_im = c_re - a_re * norm, c_im - a_im * norm
    q_re = e_re - (a_re * d_re + a_im * d_im)
    q_im = e_im - (a_im * d_re - a_re * d_im)
    num_re = g_re * p_re + g_im * p_im - q_re
    num_im = g_re * p_im - g_im * p_re - q_im
    denom = tail - (g_re * d_re + g_im * d_im)
    y_re, y_im = num_re / denom, num_im / denom
    x_re = a_re + y_re * g_re - y_im * g_im
    x_im = a_im + y_re * g_im + y_im * g_re
    half = image.shape[-2] // 2
    s_re, s_im = start[..., :half, :], start[..., half:, :]
    i_re, i_im = image[..., :half, :], image[..., half:, :]
    out_re = x_re * s_re - x_im * s_im - (y_re * i_re - y_im * i_im)
    out_im = x_re * s_im + x_im * s_re - (y_re * i_im + y_im * i_re)
    out = jnp.stack([out_re, out_im], axis=-3).astype(jnp.bfloat16)
    return out[None]


def solution(mesh):
    cores = 2
    fine = Mesh(
        mesh.devices.reshape((mesh.shape["ta"] // cores, cores) + mesh.devices.shape[1:]),
        ALL_AXES,
    )
    return jax.shard_map(
        local,
        mesh=fine,
        in_specs=(
            P(ALL_AXES, None, None, None),
            P(None, None, "gy", "gz", TIME_AXES, None, None),
            P(ALL_AXES),
            P(ALL_AXES),
        ),
        out_specs=P(None, "gy", "gz", TIME_AXES, None, None, None),
        check_vma=False,
    )
```

```python
import jax
import jax.numpy as jnp
from jax import lax
from jax.experimental import pallas as pl
from jax.experimental.pallas import tpu as pltpu
from jax.sharding import Mesh, PartitionSpec as P

ALL_AXES = ("ty", "tc", "gz", "gy")
TIME_AXES = ("ty", "tc")
SLOT_ROWS = 16
SITES = 8
BITS = (4, 2, 1)
LOW = tuple(tuple(s for s in range(SITES) if not s & bit) for bit in BITS)
HIGH = tuple(tuple(s for s in range(SITES) if s & bit) for bit in BITS)
VMEM_LIMIT = 24 * 1024 * 1024
WHOLE = pl.BlockSpec(memory_space=pltpu.VMEM)
SCALARS = pl.BlockSpec(memory_space=pltpu.SMEM)


def call(body, outs, ins, cost=None, scratch=()):
    return pl.pallas_call(
        body,
        out_shape=outs,
        in_specs=ins,
        out_specs=[WHOLE] * len(outs),
        scratch_shapes=scratch,
        cost_estimate=cost,
        compiler_params=pltpu.CompilerParams(vmem_limit_bytes=VMEM_LIMIT),
    )


def shape_of(shape, dtype):
    return jax.ShapeDtypeStruct(shape, dtype)


def shifted(values, axes, step):
    count = lax.axis_size(axes)
    return lax.ppermute(values, axes, [(i, (i + step) % count) for i in range(count)])


def pack_body(owners, slots, rows, payload):
    count, depth = rows.shape[0], rows.shape[1]
    for j in range(count):
        to = owners[j]
        payload[to, 0:depth, :] = rows[j]
        mark = jnp.full((SLOT_ROWS, rows.shape[2]), slots[j].astype(jnp.float32))
        payload[to, depth : depth + SLOT_ROWS, :] = mark.astype(payload.dtype)


def pack(rows, owners, slots):
    count, depth, width = rows.shape
    return call(
        pack_body,
        [shape_of((count, depth + SLOT_ROWS, width), rows.dtype)],
        [SCALARS, SCALARS, WHOLE],
    )(owners, slots, rows)[0]


def cut_faces(field, faces):
    for axis in range(3):
        for f in range(4):
            faces[2 * axis][f] = field[LOW[axis][f]]
            faces[2 * axis + 1][f] = field[HIGH[axis][f]]


def place_body(landed, field, *faces):
    depth = field.shape[1]
    for j in range(SITES):
        mark = landed[j, depth : depth + SLOT_ROWS, 0:128].astype(jnp.float32)
        slot = jnp.max(mark).astype(jnp.int32)
        field[slot] = landed[j, 0:depth, :]
    cut_faces(field, faces)


def place(landed):
    count, depth, width = landed.shape
    depth = depth - SLOT_ROWS
    face = shape_of((4, depth, width), landed.dtype)
    out = call(place_body, [shape_of((count, depth, width), landed.dtype)] + [face] * 6, [WHOLE])(landed)
    return out[0], out[1:]


def exchange(faces):
    (low_y, high_y, low_z, high_z, low_t, high_t) = faces
    before_z = shifted(high_z, "gz", 1)
    before_y = shifted(high_y, "gy", 1)
    behind_z = shifted(low_z, "gz", -1)
    behind_y = shifted(low_y, "gy", -1)
    before_t = shifted(high_t, TIME_AXES, 1)
    behind_t = shifted(low_t, TIME_AXES, -1)
    return [before_y, behind_y, before_z, behind_z, before_t, behind_t]


def near_body(inside, field, out):
    for s in range(SITES):
        own = field[s]
        operand = jnp.concatenate([own, own, own] + [field[s ^ bit] for bit in BITS], axis=0)
        out[s] = jnp.dot(inside[s], operand, preferred_element_type=jnp.float32)


def near(inside, field):
    count, depth, width = field.shape
    cost = pl.CostEstimate(
        flops=2 * count * depth * 6 * depth * width, bytes_accessed=4 * 2**20, transcendentals=0
    )
    return call(near_body, [shape_of(field.shape, jnp.float32)], [WHOLE, WHOLE], cost)(inside, field)[0]


def far_operand(s, received):
    parts = []
    for axis, bit in enumerate(BITS):
        if s & bit:
            parts.append(received[2 * axis + 1][HIGH[axis].index(s)])
        else:
            parts.append(received[2 * axis][LOW[axis].index(s)])
    return jnp.concatenate(parts, axis=0)


def image_body(outside, partial, r0, r1, r2, r3, r4, r5, image, field, *faces):
    received = (r0, r1, r2, r3, r4, r5)
    for s in range(SITES):
        total = partial[s] + jnp.dot(
            outside[s], far_operand(s, received), preferred_element_type=jnp.float32
        )
        image[s] = total
        field[s] = total.astype(field.dtype)
    cut_faces(field, faces)


def first_image(outside, partial, received):
    count, depth, width = partial.shape
    dtype = received[0].dtype
    outs = [shape_of(partial.shape, jnp.float32), shape_of(partial.shape, dtype)]
    outs += [shape_of((4, depth, width), dtype)] * 6
    out = call(image_body, outs, [WHOLE] * 8)(outside, partial, *received)
    return out[0], out[1], out[2:]


def fold(values):
    return jnp.sum(values.reshape((values.shape[0] // 8, 8, values.shape[1])), axis=0)


def sums_body(outside, partial, r0, r1, r2, r3, r4, r5, image, source, out):
    received = (r0, r1, r2, r3, r4, r5)
    half = image.shape[1] // 2
    sums = [jnp.zeros((8, image.shape[2]), jnp.float32) for _ in range(8)]
    for s in range(SITES):
        second = partial[s] + jnp.dot(
            outside[s], far_operand(s, received), preferred_element_type=jnp.float32
        )
        first = image[s]
        start = source[s].astype(jnp.float32)
        w_re, w_im = second[:half], second[half:]
        i_re, i_im = first[:half], first[half:]
        s_re, s_im = start[:half], start[half:]
        terms = (
            i_re * i_re + i_im * i_im,
            i_re * s_re + i_im * s_im,
            i_re * s_im - i_im * s_re,
            i_re * w_re + i_im * w_im,
            i_re * w_im - i_im * w_re,
            w_re * s_re + w_im * s_im,
            w_re * s_im - w_im * s_re,
            w_re * w_re + w_im * w_im,
        )
        sums = [a + fold(b) for a, b in zip(sums, terms)]
    rows = jnp.concatenate([jnp.sum(a, axis=0, keepdims=True) for a in sums], axis=0)
    for i in range(out.shape[0]):
        out[i] = rows


def local_sums(outside, partial, received, image, source, copies):
    width = image.shape[2]
    return call(sums_body, [shape_of((copies, 8, width), jnp.float32)], [WHOLE] * 10)(
        outside, partial, *received, image, source
    )[0]


def combine_body(landed, image, source, out):
    half = image.shape[1] // 2
    totals = jnp.sum(landed[...], axis=0)
    norm, c_re, c_im, d_re, d_im, e_re, e_im, tail = [totals[i : i + 1] for i in range(8)]
    a_re, a_im = c_re / norm, c_im / norm
    g_re, g_im = d_re / norm, d_im / norm
    p_re, p_im = c_re - a_re * norm, c_im - a_im * norm
    q_re = e_re - (a_re * d_re + a_im * d_im)
    q_im = e_im - (a_im * d_re - a_re * d_im)
    num_re = g_re * p_re + g_im * p_im - q_re
    num_im = g_re * p_im - g_im * p_re - q_im
    denom = tail - (g_re * d_re + g_im * d_im)
    y_re, y_im = num_re / denom, num_im / denom
    x_re = a_re + y_re * g_re - y_im * g_im
    x_im = a_im + y_re * g_im + y_im * g_re
    for s in range(SITES):
        first = image[s]
        start = source[s].astype(jnp.float32)
        i_re, i_im = first[:half], first[half:]
        s_re, s_im = start[:half], start[half:]
        out_re = x_re * s_re - x_im * s_im - (y_re * i_re - y_im * i_im)
        out_im = x_re * s_im + x_im * s_re - (y_re * i_im + y_im * i_re)
        out[s, 0:half, :] = out_re.astype(out.dtype)
        out[s, half:, :] = out_im.astype(out.dtype)


def combine(landed, image, source):
    return call(combine_body, [shape_of(source.shape, source.dtype)], [WHOLE] * 3)(
        landed, image, source
    )[0]


def block_double(blocks):
    columns = blocks.shape[-1] // 2
    real_blk = blocks[..., :columns]
    imag_blk = blocks[..., columns:]
    upper = jnp.concatenate([real_blk, -imag_blk], axis=-1)
    lower = jnp.concatenate([imag_blk, real_blk], axis=-1)
    return jnp.concatenate([upper, lower], axis=-2)


def split_couplings(doubled):
    inside = [doubled[0], doubled[1], doubled[2]]
    outside = []
    for dim in range(3):
        ahead, behind = doubled[3 + 2 * dim], doubled[4 + 2 * dim]
        pick = lambda a, s: lax.slice_in_dim(a, s, s + 1, axis=dim)
        inside.append(jnp.concatenate([pick(ahead, 0), pick(behind, 1)], axis=dim))
        outside.append(jnp.concatenate([pick(behind, 0), pick(ahead, 1)], axis=dim))
    flat = lambda a: a.reshape((SITES,) + a.shape[-2:])
    return flat(jnp.concatenate(inside, axis=-1)), flat(jnp.concatenate(outside, axis=-1))


def everyone(parts, axes):
    return lax.all_to_all(parts, axes, split_axis=0, concat_axis=0, tiled=True)


def local(restricted, couplings, owners, coarse_site):
    count, width = restricted.shape[0], restricted.shape[-1]
    rows = restricted.reshape(count, -1, width)
    landed = everyone(pack(rows, owners, coarse_site), "gz")
    inside, outside = split_couplings(block_double(couplings[:, 0]))
    source, faces = place(landed)
    received = exchange(faces)
    image, field, faces = first_image(outside, near(inside, source), received)
    received = exchange(faces)
    group, rest = ("tc", "gz"), ("ty", "gy")
    parts = local_sums(
        outside, near(inside, field), received, image, source, lax.axis_size(group)
    )
    parts = jnp.sum(everyone(parts, group), axis=0)
    parts = jnp.broadcast_to(parts[None], (lax.axis_size(rest),) + parts.shape)
    out = combine(everyone(parts, rest), image, source)
    return out.reshape(couplings.shape[1:5] + restricted.shape[1:])


def solution(mesh):
    cores = 2
    fine = Mesh(
        mesh.devices.reshape((mesh.shape["ta"] // cores, cores) + mesh.devices.shape[1:]),
        ALL_AXES,
    )
    return jax.shard_map(
        local,
        mesh=fine,
        in_specs=(
            P(ALL_AXES, None, None, None),
            P(None, None, "gy", "gz", TIME_AXES, None, None),
            P(ALL_AXES),
            P(ALL_AXES),
        ),
        out_specs=P(None, "gy", "gz", TIME_AXES, None, None, None),
        check_vma=False,
    )
```

```python
import jax
import jax.numpy as jnp
from jax import lax
from jax.experimental import pallas as pl
from jax.experimental.pallas import tpu as pltpu
from jax.sharding import Mesh, PartitionSpec as P

ALL_AXES = ("ya", "yb", "tc", "gz", "gy")
TIME_AXES = ("ya", "yb", "tc")
SLOT_ROWS = 16
SITES = 8
BITS = (4, 2, 1)
LOW = tuple(tuple(s for s in range(SITES) if not s & bit) for bit in BITS)
HIGH = tuple(tuple(s for s in range(SITES) if s & bit) for bit in BITS)
VMEM_LIMIT = 24 * 1024 * 1024
WHOLE = pl.BlockSpec(memory_space=pltpu.VMEM)
IN_HBM = pl.BlockSpec(memory_space=pltpu.HBM)


def call(body, outs, ins, cost=None, scratch=(), out_spec=WHOLE):
    return pl.pallas_call(
        body,
        out_shape=outs,
        in_specs=ins,
        out_specs=[out_spec] * len(outs),
        scratch_shapes=scratch,
        cost_estimate=cost,
        compiler_params=pltpu.CompilerParams(vmem_limit_bytes=VMEM_LIMIT),
    )


def shape_of(shape, dtype):
    return jax.ShapeDtypeStruct(shape, dtype)


def shifted(values, axes, step):
    count = lax.axis_size(axes)
    return lax.ppermute(values, axes, [(i, (i + step) % count) for i in range(count)])


def pack_body(owners, slots, rows, payload, owner_mem, slot_mem, row_mem, sems):
    count, depth, width = rows.shape
    copies = [
        pltpu.make_async_copy(owners, owner_mem, sems.at[0]),
        pltpu.make_async_copy(slots, slot_mem, sems.at[1]),
        pltpu.make_async_copy(rows, row_mem, sems.at[2]),
    ]
    for copy in copies:
        copy.start()
    for copy in copies:
        copy.wait()
    for j in range(count):
        to = owner_mem[j]
        payload[to, 0:depth, :] = row_mem[j]
        mark = jnp.full((SLOT_ROWS, width), slot_mem[j].astype(jnp.float32))
        payload[to, depth : depth + SLOT_ROWS, :] = mark.astype(payload.dtype)


def pack(rows, owners, slots):
    count, depth, width = rows.shape
    return call(
        pack_body,
        [shape_of((count, depth + SLOT_ROWS, width), rows.dtype)],
        [IN_HBM] * 3,
        scratch=[
            pltpu.SMEM(owners.shape, owners.dtype),
            pltpu.SMEM(slots.shape, slots.dtype),
            pltpu.VMEM(rows.shape, rows.dtype),
            pltpu.SemaphoreType.DMA((3,)),
        ],
    )(owners, slots, rows)[0]


def cut_faces(field, faces):
    for axis in range(3):
        for f in range(4):
            faces[2 * axis][f] = field[LOW[axis][f]]
            faces[2 * axis + 1][f] = field[HIGH[axis][f]]


def place_body(landed, field, *faces):
    depth = field.shape[1]
    for j in range(SITES):
        mark = landed[j, depth : depth + SLOT_ROWS, 0:128].astype(jnp.float32)
        slot = jnp.max(mark).astype(jnp.int32)
        field[slot] = landed[j, 0:depth, :]
    cut_faces(field, faces)


def place(landed):
    count, depth, width = landed.shape
    depth = depth - SLOT_ROWS
    face = shape_of((4, depth, width), landed.dtype)
    out = call(place_body, [shape_of((count, depth, width), landed.dtype)] + [face] * 6, [WHOLE])(landed)
    return out[0], out[1:]


def exchange(faces):
    (low_y, high_y, low_z, high_z, low_t, high_t) = faces
    before_z = shifted(high_z, "gz", 1)
    before_y = shifted(high_y, "gy", 1)
    behind_z = shifted(low_z, "gz", -1)
    behind_y = shifted(low_y, "gy", -1)
    before_t = shifted(high_t, TIME_AXES, 1)
    behind_t = shifted(low_t, TIME_AXES, -1)
    return [before_y, behind_y, before_z, behind_z, before_t, behind_t]


def near_product(s, inside, field):
    own = field[s]
    operand = jnp.concatenate([own, own, own] + [field[s ^ bit] for bit in BITS], axis=0)
    return jnp.dot(inside[s], operand, preferred_element_type=jnp.float32)


def near_body(inside, field, out):
    for s in range(SITES):
        out[s] = near_product(s, inside, field)


def near_cost(field):
    count, depth, width = field.shape
    return pl.CostEstimate(
        flops=2 * count * depth * 6 * depth * width, bytes_accessed=4 * 2**20, transcendentals=0
    )


def near(inside, field):
    return call(near_body, [shape_of(field.shape, jnp.float32)], [WHOLE] * 2, near_cost(field))(
        inside, field
    )[0]


def fold(values):
    return jnp.sum(values.reshape((values.shape[0] // 8, 8, values.shape[1])), axis=0)


def row_sums(sums):
    return jnp.concatenate([jnp.sum(a, axis=0, keepdims=True) for a in sums], axis=0)


def halves(values):
    half = values.shape[0] // 2
    return values[:half], values[half:]


def near_sums_body(inside, field, image, source, out, early):
    sums = [jnp.zeros((8, image.shape[2]), jnp.float32) for _ in range(3)]
    for s in range(SITES):
        out[s] = near_product(s, inside, field)
        i_re, i_im = halves(image[s])
        s_re, s_im = halves(source[s].astype(jnp.float32))
        terms = (
            i_re * i_re + i_im * i_im,
            i_re * s_re + i_im * s_im,
            i_re * s_im - i_im * s_re,
        )
        sums = [a + fold(b) for a, b in zip(sums, terms)]
    early[...] = row_sums(sums + [jnp.zeros((8, image.shape[2]), jnp.float32)] * 5)


def near_sums(inside, field, image, source):
    outs = [shape_of(field.shape, jnp.float32), shape_of((8, field.shape[2]), jnp.float32)]
    return call(near_sums_body, outs, [WHOLE] * 4, near_cost(field))(inside, field, image, source)


def far_operand(s, received):
    parts = []
    for axis, bit in enumerate(BITS):
        if s & bit:
            parts.append(received[2 * axis + 1][HIGH[axis].index(s)])
        else:
            parts.append(received[2 * axis][LOW[axis].index(s)])
    return jnp.concatenate(parts, axis=0)


def image_body(outside, partial, r0, r1, r2, r3, r4, r5, image, field, *faces):
    received = (r0, r1, r2, r3, r4, r5)
    for s in range(SITES):
        total = partial[s] + jnp.dot(
            outside[s], far_operand(s, received), preferred_element_type=jnp.float32
        )
        image[s] = total
        field[s] = total.astype(field.dtype)
    cut_faces(field, faces)


def first_image(outside, partial, received):
    count, depth, width = partial.shape
    dtype = received[0].dtype
    outs = [shape_of(partial.shape, jnp.float32), shape_of(partial.shape, dtype)]
    outs += [shape_of((4, depth, width), dtype)] * 6
    out = call(image_body, outs, [WHOLE] * 8)(outside, partial, *received)
    return out[0], out[1], out[2:]


def sums_body(outside, partial, early, r0, r1, r2, r3, r4, r5, image, source, out):
    received = (r0, r1, r2, r3, r4, r5)
    sums = [jnp.zeros((8, image.shape[2]), jnp.float32) for _ in range(5)]
    for s in range(SITES):
        second = partial[s] + jnp.dot(
            outside[s], far_operand(s, received), preferred_element_type=jnp.float32
        )
        w_re, w_im = halves(second)
        i_re, i_im = halves(image[s])
        s_re, s_im = halves(source[s].astype(jnp.float32))
        terms = (
            i_re * w_re + i_im * w_im,
            i_re * w_im - i_im * w_re,
            w_re * s_re + w_im * s_im,
            w_re * s_im - w_im * s_re,
            w_re * w_re + w_im * w_im,
        )
        sums = [a + fold(b) for a, b in zip(sums, terms)]
    nothing = jnp.zeros((8, image.shape[2]), jnp.float32)
    out[...] = early[...] + row_sums([nothing] * 3 + sums)


def local_sums(outside, partial, early, received, image, source):
    return call(sums_body, [shape_of(early.shape, early.dtype)], [WHOLE] * 11)(
        outside, partial, early, *received, image, source
    )[0]


def combine_body(landed, image, source, out, held, sems):
    half = image.shape[1] // 2
    copies = []
    totals = jnp.sum(landed[...], axis=0)
    norm, c_re, c_im, d_re, d_im, e_re, e_im, tail = [totals[i : i + 1] for i in range(8)]
    a_re, a_im = c_re / norm, c_im / norm
    g_re, g_im = d_re / norm, d_im / norm
    p_re, p_im = c_re - a_re * norm, c_im - a_im * norm
    q_re = e_re - (a_re * d_re + a_im * d_im)
    q_im = e_im - (a_im * d_re - a_re * d_im)
    num_re = g_re * p_re + g_im * p_im - q_re
    num_im = g_re * p_im - g_im * p_re - q_im
    denom = tail - (g_re * d_re + g_im * d_im)
    y_re, y_im = num_re / denom, num_im / denom
    x_re = a_re + y_re * g_re - y_im * g_im
    x_im = a_im + y_re * g_im + y_im * g_re
    for s in range(SITES):
        i_re, i_im = halves(image[s])
        s_re, s_im = halves(source[s].astype(jnp.float32))
        out_re = x_re * s_re - x_im * s_im - (y_re * i_re - y_im * i_im)
        out_im = x_re * s_im + x_im * s_re - (y_re * i_im + y_im * i_re)
        held[s, 0:half, :] = out_re.astype(held.dtype)
        held[s, half:, :] = out_im.astype(held.dtype)
        copies.append(pltpu.make_async_copy(held.at[s], out.at[s], sems.at[s]))
        copies[s].start()
    for copy in copies:
        copy.wait()


def combine(landed, image, source):
    return call(
        combine_body,
        [shape_of(source.shape, source.dtype)],
        [WHOLE] * 3,
        scratch=[pltpu.VMEM(source.shape, source.dtype), pltpu.SemaphoreType.DMA((SITES,))],
        out_spec=IN_HBM,
    )(landed, image, source)[0]


def block_double(blocks):
    columns = blocks.shape[-1] // 2
    real_blk = blocks[..., :columns]
    imag_blk = blocks[..., columns:]
    upper = jnp.concatenate([real_blk, -imag_blk], axis=-1)
    lower = jnp.concatenate([imag_blk, real_blk], axis=-1)
    return jnp.concatenate([upper, lower], axis=-2)


def split_couplings(doubled):
    inside = [doubled[0], doubled[1], doubled[2]]
    outside = []
    for dim in range(3):
        ahead, behind = doubled[3 + 2 * dim], doubled[4 + 2 * dim]
        pick = lambda a, s: lax.slice_in_dim(a, s, s + 1, axis=dim)
        inside.append(jnp.concatenate([pick(ahead, 0), pick(behind, 1)], axis=dim))
        outside.append(jnp.concatenate([pick(behind, 0), pick(ahead, 1)], axis=dim))
    flat = lambda a: a.reshape((SITES,) + a.shape[-2:])
    return flat(jnp.concatenate(inside, axis=-1)), flat(jnp.concatenate(outside, axis=-1))


def copies_of(parts, axes):
    return jnp.broadcast_to(parts[None], (lax.axis_size(axes),) + parts.shape)


def everyone(parts, axes):
    return lax.all_to_all(parts, axes, split_axis=0, concat_axis=0, tiled=True)


def local(restricted, couplings, owners, coarse_site):
    count, width = restricted.shape[0], restricted.shape[-1]
    rows = restricted.reshape(count, -1, width)
    landed = everyone(pack(rows, owners, coarse_site), "gz")
    inside, outside = split_couplings(block_double(couplings[:, 0]))
    source, faces = place(landed)
    received = exchange(faces)
    image, field, faces = first_image(outside, near(inside, source), received)
    received = exchange(faces)
    partial, early = near_sums(inside, field, image, source)
    parts = local_sums(outside, partial, early, received, image, source)
    parts = jnp.sum(lax.all_gather(parts, "tc"), axis=0)
    parts = jnp.sum(everyone(copies_of(parts, ("yb", "gz")), ("yb", "gz")), axis=0)
    parts = everyone(copies_of(parts, ("ya", "gy")), ("ya", "gy"))
    out = combine(parts, image, source)
    return out.reshape(couplings.shape[1:5] + restricted.shape[1:])


def solution(mesh):
    count = mesh.shape["ta"]
    fine = Mesh(mesh.devices.reshape((count // 4, 2, 2) + mesh.devices.shape[1:]), ALL_AXES)
    return jax.shard_map(
        local,
        mesh=fine,
        in_specs=(
            P(ALL_AXES, None, None, None),
            P(None, None, "gy", "gz", TIME_AXES, None, None),
            P(ALL_AXES),
            P(ALL_AXES),
        ),
        out_specs=P(None, "gy", "gz", TIME_AXES, None, None, None),
        check_vma=False,
    )
```

```python
import jax
import jax.numpy as jnp
from jax import lax
from jax.experimental import pallas as pl
from jax.experimental.pallas import tpu as pltpu
from jax.sharding import Mesh, PartitionSpec as P

ALL_AXES = ("ya", "yb", "tc", "gz", "gy")
TIME_AXES = ("ya", "yb", "tc")
SLOT_ROWS = 16
SITES = 8
BITS = (4, 2, 1)
LOW = tuple(tuple(s for s in range(SITES) if not s & bit) for bit in BITS)
HIGH = tuple(tuple(s for s in range(SITES) if s & bit) for bit in BITS)
VMEM_LIMIT = 24 * 1024 * 1024
PACK_LIMIT = 60 * 1024 * 1024
WHOLE = pl.BlockSpec(memory_space=pltpu.VMEM)
IN_HBM = pl.BlockSpec(memory_space=pltpu.HBM)


def call(body, outs, ins, cost=None, scratch=(), out_spec=WHOLE, limit=VMEM_LIMIT):
    return pl.pallas_call(
        body,
        out_shape=outs,
        in_specs=ins,
        out_specs=[out_spec] * len(outs),
        scratch_shapes=scratch,
        cost_estimate=cost,
        compiler_params=pltpu.CompilerParams(vmem_limit_bytes=limit),
    )


def shape_of(shape, dtype):
    return jax.ShapeDtypeStruct(shape, dtype)


def shifted(values, axes, step):
    count = lax.axis_size(axes)
    return lax.ppermute(values, axes, [(i, (i + step) % count) for i in range(count)])


def pack_body(owners, slots, rows, payload, owner_mem, slot_mem, row_mem, sems):
    count, depth, width = rows.shape
    copies = [
        pltpu.make_async_copy(owners, owner_mem, sems.at[0]),
        pltpu.make_async_copy(slots, slot_mem, sems.at[1]),
        pltpu.make_async_copy(rows, row_mem, sems.at[2]),
    ]
    for copy in copies:
        copy.start()
    for copy in copies:
        copy.wait()
    for j in range(count):
        to = owner_mem[j]
        payload[to, 0:depth, :] = row_mem[j]
        mark = jnp.full((SLOT_ROWS, width), slot_mem[j].astype(jnp.float32))
        payload[to, depth : depth + SLOT_ROWS, :] = mark.astype(payload.dtype)


def pack(rows, owners, slots):
    count, depth, width = rows.shape
    return call(
        pack_body,
        [shape_of((count, depth + SLOT_ROWS, width), rows.dtype)],
        [IN_HBM] * 3,
        scratch=[
            pltpu.SMEM(owners.shape, owners.dtype),
            pltpu.SMEM(slots.shape, slots.dtype),
            pltpu.VMEM(rows.shape, rows.dtype),
            pltpu.SemaphoreType.DMA((3,)),
        ],
        limit=PACK_LIMIT,
    )(owners, slots, rows)[0]


def cut_faces(field, faces):
    for axis in range(3):
        for f in range(4):
            faces[2 * axis][f] = field[LOW[axis][f]]
            faces[2 * axis + 1][f] = field[HIGH[axis][f]]


def place_body(landed, field, *faces):
    depth = field.shape[1]
    for j in range(SITES):
        mark = landed[j, depth : depth + SLOT_ROWS, 0:128].astype(jnp.float32)
        slot = jnp.max(mark).astype(jnp.int32)
        field[slot] = landed[j, 0:depth, :]
    cut_faces(field, faces)


def place(landed):
    count, depth, width = landed.shape
    depth = depth - SLOT_ROWS
    face = shape_of((4, depth, width), landed.dtype)
    out = call(place_body, [shape_of((count, depth, width), landed.dtype)] + [face] * 6, [WHOLE])(landed)
    return out[0], out[1:]


def exchange(faces):
    (low_y, high_y, low_z, high_z, low_t, high_t) = faces
    before_z = shifted(high_z, "gz", 1)
    before_y = shifted(high_y, "gy", 1)
    behind_z = shifted(low_z, "gz", -1)
    behind_y = shifted(low_y, "gy", -1)
    before_t = shifted(high_t, TIME_AXES, 1)
    behind_t = shifted(low_t, TIME_AXES, -1)
    return [before_y, behind_y, before_z, behind_z, before_t, behind_t]


def near_product(s, inside, field):
    own = field[s]
    operand = jnp.concatenate([own, own, own] + [field[s ^ bit] for bit in BITS], axis=0)
    return jnp.dot(inside[s], operand, preferred_element_type=jnp.float32)


def near_body(inside, field, out):
    for s in range(SITES):
        out[s] = near_product(s, inside, field)


def near_cost(field):
    count, depth, width = field.shape
    return pl.CostEstimate(
        flops=2 * count * depth * 6 * depth * width, bytes_accessed=4 * 2**20, transcendentals=0
    )


def near(inside, field):
    return call(near_body, [shape_of(field.shape, jnp.float32)], [WHOLE] * 2, near_cost(field))(
        inside, field
    )[0]


def fold(values):
    return jnp.sum(values.reshape((values.shape[0] // 8, 8, values.shape[1])), axis=0)


def row_sums(sums):
    return jnp.concatenate([jnp.sum(a, axis=0, keepdims=True) for a in sums], axis=0)


def halves(values):
    half = values.shape[0] // 2
    return values[:half], values[half:]


def near_sums_body(inside, field, image, source, out, early):
    sums = [jnp.zeros((8, image.shape[2]), jnp.float32) for _ in range(3)]
    for s in range(SITES):
        out[s] = near_product(s, inside, field)
        i_re, i_im = halves(image[s])
        s_re, s_im = halves(source[s].astype(jnp.float32))
        terms = (
            i_re * i_re + i_im * i_im,
            i_re * s_re + i_im * s_im,
            i_re * s_im - i_im * s_re,
        )
        sums = [a + fold(b) for a, b in zip(sums, terms)]
    early[...] = row_sums(sums + [jnp.zeros((8, image.shape[2]), jnp.float32)] * 5)


def near_sums(inside, field, image, source):
    outs = [shape_of(field.shape, jnp.float32), shape_of((8, field.shape[2]), jnp.float32)]
    return call(near_sums_body, outs, [WHOLE] * 4, near_cost(field))(inside, field, image, source)


def far_operand(s, received):
    parts = []
    for axis, bit in enumerate(BITS):
        if s & bit:
            parts.append(received[2 * axis + 1][HIGH[axis].index(s)])
        else:
            parts.append(received[2 * axis][LOW[axis].index(s)])
    return jnp.concatenate(parts, axis=0)


def image_body(outside, partial, r0, r1, r2, r3, r4, r5, image, field, *faces):
    received = (r0, r1, r2, r3, r4, r5)
    for s in range(SITES):
        total = partial[s] + jnp.dot(
            outside[s], far_operand(s, received), preferred_element_type=jnp.float32
        )
        image[s] = total
        field[s] = total.astype(field.dtype)
    cut_faces(field, faces)


def first_image(outside, partial, received):
    count, depth, width = partial.shape
    dtype = received[0].dtype
    outs = [shape_of(partial.shape, jnp.float32), shape_of(partial.shape, dtype)]
    outs += [shape_of((4, depth, width), dtype)] * 6
    out = call(image_body, outs, [WHOLE] * 8)(outside, partial, *received)
    return out[0], out[1], out[2:]


def sums_body(outside, partial, early, r0, r1, r2, r3, r4, r5, image, source, out):
    received = (r0, r1, r2, r3, r4, r5)
    sums = [jnp.zeros((8, image.shape[2]), jnp.float32) for _ in range(5)]
    for s in range(SITES):
        second = partial[s] + jnp.dot(
            outside[s], far_operand(s, received), preferred_element_type=jnp.float32
        )
        w_re, w_im = halves(second)
        i_re, i_im = halves(image[s])
        s_re, s_im = halves(source[s].astype(jnp.float32))
        terms = (
            i_re * w_re + i_im * w_im,
            i_re * w_im - i_im * w_re,
            w_re * s_re + w_im * s_im,
            w_re * s_im - w_im * s_re,
            w_re * w_re + w_im * w_im,
        )
        sums = [a + fold(b) for a, b in zip(sums, terms)]
    nothing = jnp.zeros((8, image.shape[2]), jnp.float32)
    out[...] = early[...] + row_sums([nothing] * 3 + sums)


def local_sums(outside, partial, early, received, image, source):
    return call(sums_body, [shape_of(early.shape, early.dtype)], [WHOLE] * 11)(
        outside, partial, early, *received, image, source
    )[0]


def combine_body(landed, image, source, out, held, sems):
    half = image.shape[1] // 2
    copies = []
    totals = jnp.sum(landed[...], axis=0)
    norm, c_re, c_im, d_re, d_im, e_re, e_im, tail = [totals[i : i + 1] for i in range(8)]
    a_re, a_im = c_re / norm, c_im / norm
    g_re, g_im = d_re / norm, d_im / norm
    p_re, p_im = c_re - a_re * norm, c_im - a_im * norm
    q_re = e_re - (a_re * d_re + a_im * d_im)
    q_im = e_im - (a_im * d_re - a_re * d_im)
    num_re = g_re * p_re + g_im * p_im - q_re
    num_im = g_re * p_im - g_im * p_re - q_im
    denom = tail - (g_re * d_re + g_im * d_im)
    y_re, y_im = num_re / denom, num_im / denom
    x_re = a_re + y_re * g_re - y_im * g_im
    x_im = a_im + y_re * g_im + y_im * g_re
    for s in range(SITES):
        i_re, i_im = halves(image[s])
        s_re, s_im = halves(source[s].astype(jnp.float32))
        out_re = x_re * s_re - x_im * s_im - (y_re * i_re - y_im * i_im)
        out_im = x_re * s_im + x_im * s_re - (y_re * i_im + y_im * i_re)
        held[s, 0:half, :] = out_re.astype(held.dtype)
        held[s, half:, :] = out_im.astype(held.dtype)
        copies.append(pltpu.make_async_copy(held.at[s], out.at[s], sems.at[s]))
        copies[s].start()
    for copy in copies:
        copy.wait()


def combine(landed, image, source):
    return call(
        combine_body,
        [shape_of(source.shape, source.dtype)],
        [WHOLE] * 3,
        scratch=[pltpu.VMEM(source.shape, source.dtype), pltpu.SemaphoreType.DMA((SITES,))],
        out_spec=IN_HBM,
    )(landed, image, source)[0]


def split_body(couplings, inside, outside):
    half, width = couplings.shape[2], couplings.shape[3]
    real_lanes = lax.broadcasted_iota(jnp.int32, (half, width), 1) < width // 2

    def put(target, s, j, k):
        block = couplings[k, s].astype(jnp.float32)
        upper = jnp.where(real_lanes, block, -block)
        lower = pltpu.roll(block, width // 2, 1)
        target[s, 0:half, j * width : (j + 1) * width] = upper.astype(target.dtype)
        target[s, half:, j * width : (j + 1) * width] = lower.astype(target.dtype)

    for s in range(SITES):
        for k in range(3):
            put(inside, s, k, k)
        for axis, bit in enumerate(BITS):
            ahead, behind = 3 + 2 * axis, 4 + 2 * axis
            put(inside, s, 3 + axis, behind if s & bit else ahead)
            put(outside, s, axis, ahead if s & bit else behind)


def split_couplings(couplings):
    blocks = couplings.reshape((couplings.shape[0], SITES) + couplings.shape[-2:])
    width = blocks.shape[-1]
    outs = [shape_of((SITES, width, n * width), blocks.dtype) for n in (6, 3)]
    return call(split_body, outs, [WHOLE])(blocks)


def copies_of(parts, axes):
    return jnp.broadcast_to(parts[None], (lax.axis_size(axes),) + parts.shape)


def everyone(parts, axes):
    return lax.all_to_all(parts, axes, split_axis=0, concat_axis=0, tiled=True)


def local(restricted, couplings, owners, coarse_site):
    count, width = restricted.shape[0], restricted.shape[-1]
    rows = restricted.reshape(count, -1, width)
    landed = everyone(pack(rows, owners, coarse_site), "gz")
    landed, inside, outside = lax.optimization_barrier((landed, *split_couplings(couplings)))
    source, faces = place(landed)
    received = exchange(faces)
    image, field, faces = first_image(outside, near(inside, source), received)
    received = exchange(faces)
    partial, early = near_sums(inside, field, image, source)
    parts = local_sums(outside, partial, early, received, image, source)
    parts = jnp.sum(lax.all_gather(parts, "tc"), axis=0)
    parts = jnp.sum(everyone(copies_of(parts, ("yb", "gz")), ("yb", "gz")), axis=0)
    parts = everyone(copies_of(parts, ("ya", "gy")), ("ya", "gy"))
    out = combine(parts, image, source)
    return out.reshape(couplings.shape[1:5] + restricted.shape[1:])


def solution(mesh):
    count = mesh.shape["ta"]
    fine = Mesh(mesh.devices.reshape((count // 4, 2, 2) + mesh.devices.shape[1:]), ALL_AXES)
    return jax.shard_map(
        local,
        mesh=fine,
        in_specs=(
            P(ALL_AXES, None, None, None),
            P(None, None, "gy", "gz", TIME_AXES, None, None),
            P(ALL_AXES),
            P(ALL_AXES),
        ),
        out_specs=P(None, "gy", "gz", TIME_AXES, None, None, None),
        check_vma=False,
    )
```

```python
import jax
import jax.numpy as jnp
from jax import lax
from jax.experimental import pallas as pl
from jax.experimental.pallas import tpu as pltpu
import numpy as np
from jax.sharding import Mesh, PartitionSpec as P

ALL_AXES = ("ya", "yb", "tc", "gz", "gy")
TIME_AXES = ("ya", "yb", "tc")
TC, GZ, GY = 2, 3, 4
SLOT_ROWS = 16
LANES = 128
SITES = 8
BITS = (4, 2, 1)
LOW = tuple(tuple(s for s in range(SITES) if not s & bit) for bit in BITS)
HIGH = tuple(tuple(s for s in range(SITES) if s & bit) for bit in BITS)
VMEM_LIMIT = 24 * 1024 * 1024
PACK_LIMIT = 60 * 1024 * 1024
WHOLE = pl.BlockSpec(memory_space=pltpu.VMEM)
IN_HBM = pl.BlockSpec(memory_space=pltpu.HBM)


def call(body, outs, ins, cost=None, scratch=(), out_spec=WHOLE, limit=VMEM_LIMIT):
    return pl.pallas_call(
        body,
        out_shape=outs,
        in_specs=ins,
        out_specs=[out_spec] * len(outs),
        scratch_shapes=scratch,
        cost_estimate=cost,
        compiler_params=pltpu.CompilerParams(vmem_limit_bytes=limit),
    )


def shape_of(shape, dtype):
    return jax.ShapeDtypeStruct(shape, dtype)


def shifted(values, axes, step):
    count = lax.axis_size(axes)
    return lax.ppermute(values, axes, [(i, (i + step) % count) for i in range(count)])


def pack_body(owners, slots, rows, payload, owner_mem, slot_mem, row_mem, tail_mem, sems, out_sems):
    count, depth, width = rows.shape
    lanes = payload.shape[2]
    parts = width // lanes
    loads = [
        pltpu.make_async_copy(owners, owner_mem, sems.at[0]),
        pltpu.make_async_copy(slots, slot_mem, sems.at[1]),
        pltpu.make_async_copy(rows, row_mem, sems.at[2]),
    ]
    for load in loads:
        load.start()
    loads[0].wait()
    loads[1].wait()
    copies = []
    for j in range(count):
        mark = jnp.full((SLOT_ROWS, lanes), slot_mem[j].astype(jnp.float32))
        tail_mem[j] = mark.astype(payload.dtype)
        tail = payload.at[owner_mem[j], pl.ds(parts * depth, SLOT_ROWS)]
        copies.append(pltpu.make_async_copy(tail_mem.at[j], tail, out_sems.at[j, parts]))
        copies[-1].start()
    loads[2].wait()
    for j in range(count):
        for part in range(parts):
            block = row_mem.at[j, :, pl.ds(part * lanes, lanes)]
            place = payload.at[owner_mem[j], pl.ds(part * depth, depth)]
            copies.append(pltpu.make_async_copy(block, place, out_sems.at[j, part]))
            copies[-1].start()
    for copy in copies:
        copy.wait()


def pack(rows, owners, slots):
    count, depth, width = rows.shape
    parts = width // LANES
    return call(
        pack_body,
        [shape_of((count, parts * depth + SLOT_ROWS, LANES), rows.dtype)],
        [IN_HBM] * 3,
        scratch=[
            pltpu.SMEM(owners.shape, owners.dtype),
            pltpu.SMEM(slots.shape, slots.dtype),
            pltpu.VMEM(rows.shape, rows.dtype),
            pltpu.VMEM((count, SLOT_ROWS, LANES), rows.dtype),
            pltpu.SemaphoreType.DMA((3,)),
            pltpu.SemaphoreType.DMA((count, parts + 1)),
        ],
        out_spec=IN_HBM,
        limit=PACK_LIMIT,
    )(owners, slots, rows)[0]


def each_core(body):
    core = lax.axis_index("tc")

    @pl.when(core == 0)
    def _():
        body((1, 0))

    @pl.when(core != 0)
    def _():
        body((0, 1))


def cut_faces(field, faces):
    def cut(order):
        for place, axis in enumerate(order):
            for f in range(4):
                faces[2 * place][f] = field[HIGH[axis][f]]
                faces[2 * place + 1][f] = field[LOW[axis][f]]

    each_core(cut)
    for f in range(4):
        faces[4][f] = field[HIGH[2][f]]
        faces[5][f] = field[LOW[2][f]]


def place_body(landed, field, *faces):
    depth, width = field.shape[1], field.shape[2]
    lanes = landed.shape[2]
    parts = width // lanes
    for j in range(SITES):
        mark = landed[j, parts * depth : parts * depth + SLOT_ROWS, :].astype(jnp.float32)
        slot = jnp.max(mark).astype(jnp.int32)
        for part in range(parts):
            block = landed[j, part * depth : (part + 1) * depth, :]
            field[slot, :, part * lanes : (part + 1) * lanes] = block
    cut_faces(field, faces)


def place(landed, depth, width):
    face = shape_of((4, depth, width), landed.dtype)
    field = shape_of((landed.shape[0], depth, width), landed.dtype)
    out = call(place_body, [field] + [face] * 6, [WHOLE])(landed)
    return out[0], out[1:]


def crossed(values, first, step):
    sizes = [lax.axis_size(axis) for axis in ALL_AXES]
    pairs = []
    for start in np.ndindex(*sizes):
        to = list(start)
        axis = GZ if start[TC] == first else GY
        to[axis] = (to[axis] + step) % sizes[axis]
        pairs.append(tuple(int(np.ravel_multi_index(at, sizes)) for at in (start, to)))
    return lax.ppermute(values, ALL_AXES, pairs)


def exchange(faces):
    ahead, behind = crossed(faces[0], 0, 1), crossed(faces[1], 0, -1)
    ahead_b, behind_b = crossed(faces[2], 1, 1), crossed(faces[3], 1, -1)
    before_t = shifted(faces[4], TIME_AXES, 1)
    behind_t = shifted(faces[5], TIME_AXES, -1)
    return [ahead, behind, ahead_b, behind_b, before_t, behind_t]


def near_product(s, inside, field):
    own = field[s]
    operand = jnp.concatenate([own, own, own] + [field[s ^ bit] for bit in BITS], axis=0)
    return jnp.dot(inside[s], operand, preferred_element_type=jnp.float32)


def near_body(inside, field, out):
    for s in range(SITES):
        out[s] = near_product(s, inside, field)


def near_cost(field):
    count, depth, width = field.shape
    return pl.CostEstimate(
        flops=2 * count * depth * 6 * depth * width, bytes_accessed=4 * 2**20, transcendentals=0
    )


def near(inside, field):
    return call(near_body, [shape_of(field.shape, jnp.float32)], [WHOLE] * 2, near_cost(field))(
        inside, field
    )[0]


def fold(values):
    return jnp.sum(values.reshape((values.shape[0] // 8, 8, values.shape[1])), axis=0)


def row_sums(sums):
    return jnp.concatenate([jnp.sum(a, axis=0, keepdims=True) for a in sums], axis=0)


def halves(values):
    half = values.shape[0] // 2
    return values[:half], values[half:]


def near_sums_body(inside, field, image, source, out, early):
    sums = [jnp.zeros((8, image.shape[2]), jnp.float32) for _ in range(3)]
    for s in range(SITES):
        out[s] = near_product(s, inside, field)
        i_re, i_im = halves(image[s])
        s_re, s_im = halves(source[s].astype(jnp.float32))
        terms = (
            i_re * i_re + i_im * i_im,
            i_re * s_re + i_im * s_im,
            i_re * s_im - i_im * s_re,
        )
        sums = [a + fold(b) for a, b in zip(sums, terms)]
    early[...] = row_sums(sums + [jnp.zeros((8, image.shape[2]), jnp.float32)] * 5)


def near_sums(inside, field, image, source):
    outs = [shape_of(field.shape, jnp.float32), shape_of((8, field.shape[2]), jnp.float32)]
    return call(near_sums_body, outs, [WHOLE] * 4, near_cost(field))(inside, field, image, source)


def far_operand(s, received, order):
    parts = [None] * 3
    for place, axis in enumerate(order + (2,)):
        if s & BITS[axis]:
            parts[axis] = received[2 * place + 1][HIGH[axis].index(s)]
        else:
            parts[axis] = received[2 * place][LOW[axis].index(s)]
    return jnp.concatenate(parts, axis=0)


def image_body(outside, partial, r0, r1, r2, r3, r4, r5, image, field, *faces):
    received = (r0, r1, r2, r3, r4, r5)

    def add(order):
        for s in range(SITES):
            operand = far_operand(s, received, order)
            total = partial[s] + jnp.dot(outside[s], operand, preferred_element_type=jnp.float32)
            image[s] = total
            field[s] = total.astype(field.dtype)

    each_core(add)
    cut_faces(field, faces)


def first_image(outside, partial, received):
    count, depth, width = partial.shape
    dtype = received[0].dtype
    outs = [shape_of(partial.shape, jnp.float32), shape_of(partial.shape, dtype)]
    outs += [shape_of((4, depth, width), dtype)] * 6
    out = call(image_body, outs, [WHOLE] * 8)(outside, partial, *received)
    return out[0], out[1], out[2:]


def sums_body(outside, partial, early, r0, r1, r2, r3, r4, r5, image, source, out):
    received = (r0, r1, r2, r3, r4, r5)

    def add(order):
        sums = [jnp.zeros((8, image.shape[2]), jnp.float32) for _ in range(5)]
        for s in range(SITES):
            operand = far_operand(s, received, order)
            second = partial[s] + jnp.dot(outside[s], operand, preferred_element_type=jnp.float32)
            w_re, w_im = halves(second)
            i_re, i_im = halves(image[s])
            s_re, s_im = halves(source[s].astype(jnp.float32))
            terms = (
                i_re * w_re + i_im * w_im,
                i_re * w_im - i_im * w_re,
                w_re * s_re + w_im * s_im,
                w_re * s_im - w_im * s_re,
                w_re * w_re + w_im * w_im,
            )
            sums = [a + fold(b) for a, b in zip(sums, terms)]
        nothing = jnp.zeros((8, image.shape[2]), jnp.float32)
        out[...] = early[...] + row_sums([nothing] * 3 + sums)

    each_core(add)


def local_sums(outside, partial, early, received, image, source):
    return call(sums_body, [shape_of(early.shape, early.dtype)], [WHOLE] * 11)(
        outside, partial, early, *received, image, source
    )[0]


def combine_body(landed, image, source, out, held, sems):
    half = image.shape[1] // 2
    copies = []
    totals = jnp.sum(landed[...], axis=0)
    norm, c_re, c_im, d_re, d_im, e_re, e_im, tail = [totals[i : i + 1] for i in range(8)]
    a_re, a_im = c_re / norm, c_im / norm
    g_re, g_im = d_re / norm, d_im / norm
    p_re, p_im = c_re - a_re * norm, c_im - a_im * norm
    q_re = e_re - (a_re * d_re + a_im * d_im)
    q_im = e_im - (a_im * d_re - a_re * d_im)
    num_re = g_re * p_re + g_im * p_im - q_re
    num_im = g_re * p_im - g_im * p_re - q_im
    denom = tail - (g_re * d_re + g_im * d_im)
    y_re, y_im = num_re / denom, num_im / denom
    x_re = a_re + y_re * g_re - y_im * g_im
    x_im = a_im + y_re * g_im + y_im * g_re
    for s in range(SITES):
        i_re, i_im = halves(image[s])
        s_re, s_im = halves(source[s].astype(jnp.float32))
        out_re = x_re * s_re - x_im * s_im - (y_re * i_re - y_im * i_im)
        out_im = x_re * s_im + x_im * s_re - (y_re * i_im + y_im * i_re)
        held[s, 0:half, :] = out_re.astype(held.dtype)
        held[s, half:, :] = out_im.astype(held.dtype)
        copies.append(pltpu.make_async_copy(held.at[s], out.at[s], sems.at[s]))
        copies[s].start()
    for copy in copies:
        copy.wait()


def combine(landed, image, source):
    return call(
        combine_body,
        [shape_of(source.shape, source.dtype)],
        [WHOLE] * 3,
        scratch=[pltpu.VMEM(source.shape, source.dtype), pltpu.SemaphoreType.DMA((SITES,))],
        out_spec=IN_HBM,
    )(landed, image, source)[0]


def split_body(couplings, inside, outside):
    half, width = couplings.shape[2], couplings.shape[3]
    real_lanes = lax.broadcasted_iota(jnp.int32, (half, width), 1) < width // 2

    def put(target, s, j, k):
        block = couplings[k, s].astype(jnp.float32)
        upper = jnp.where(real_lanes, block, -block)
        lower = pltpu.roll(block, width // 2, 1)
        target[s, 0:half, j * width : (j + 1) * width] = upper.astype(target.dtype)
        target[s, half:, j * width : (j + 1) * width] = lower.astype(target.dtype)

    for s in range(SITES):
        for k in range(3):
            put(inside, s, k, k)
        for axis, bit in enumerate(BITS):
            ahead, behind = 3 + 2 * axis, 4 + 2 * axis
            put(inside, s, 3 + axis, behind if s & bit else ahead)
            put(outside, s, axis, ahead if s & bit else behind)


def split_couplings(couplings):
    blocks = couplings.reshape((couplings.shape[0], SITES) + couplings.shape[-2:])
    width = blocks.shape[-1]
    outs = [shape_of((SITES, width, n * width), blocks.dtype) for n in (6, 3)]
    return call(split_body, outs, [WHOLE])(blocks)


def copies_of(parts, axes):
    return jnp.broadcast_to(parts[None], (lax.axis_size(axes),) + parts.shape)


def everyone(parts, axes):
    return lax.all_to_all(parts, axes, split_axis=0, concat_axis=0, tiled=True)


def local(restricted, couplings, owners, coarse_site):
    count, width = restricted.shape[0], restricted.shape[-1]
    rows = restricted.reshape(count, -1, width)
    landed = everyone(pack(rows, owners, coarse_site), "gz")
    landed, inside, outside = lax.optimization_barrier((landed, *split_couplings(couplings)))
    source, faces = place(landed, rows.shape[1], width)
    received = exchange(faces)
    image, field, faces = first_image(outside, near(inside, source), received)
    received = exchange(faces)
    partial, early = near_sums(inside, field, image, source)
    parts = local_sums(outside, partial, early, received, image, source)
    parts = jnp.sum(lax.all_gather(parts, "tc"), axis=0)
    parts = jnp.sum(everyone(copies_of(parts, ("yb", "gz")), ("yb", "gz")), axis=0)
    parts = everyone(copies_of(parts, ("ya", "gy")), ("ya", "gy"))
    out = combine(parts, image, source)
    return out.reshape(couplings.shape[1:5] + restricted.shape[1:])


def solution(mesh):
    count = mesh.shape["ta"]
    fine = Mesh(mesh.devices.reshape((count // 4, 2, 2) + mesh.devices.shape[1:]), ALL_AXES)
    return jax.shard_map(
        local,
        mesh=fine,
        in_specs=(
            P(ALL_AXES, None, None, None),
            P(None, None, "gy", "gz", TIME_AXES, None, None),
            P(ALL_AXES),
            P(ALL_AXES),
        ),
        out_specs=P(None, "gy", "gz", TIME_AXES, None, None, None),
        check_vma=False,
    )
```

```python
import jax
import jax.numpy as jnp
from jax import lax
from jax.experimental import pallas as pl
from jax.experimental.pallas import tpu as pltpu
import numpy as np
from jax.sharding import Mesh, PartitionSpec as P

ALL_AXES = ("ya", "yb", "tc", "gz", "gy")
TIME_AXES = ("ya", "yb", "tc")
TC, GZ, GY = 2, 3, 4
ORDER = (0, 1, 2, 4, 3, 5)
SLOT_ROWS = 16
LANES = 128
SITES = 8
BITS = (4, 2, 1)
LOW = tuple(tuple(s for s in range(SITES) if not s & bit) for bit in BITS)
HIGH = tuple(tuple(s for s in range(SITES) if s & bit) for bit in BITS)
VMEM_LIMIT = 24 * 1024 * 1024
PACK_LIMIT = 60 * 1024 * 1024
WHOLE = pl.BlockSpec(memory_space=pltpu.VMEM)
IN_HBM = pl.BlockSpec(memory_space=pltpu.HBM)


def call(body, outs, ins, cost=None, scratch=(), out_spec=WHOLE, limit=VMEM_LIMIT):
    return pl.pallas_call(
        body,
        out_shape=outs,
        in_specs=ins,
        out_specs=[out_spec] * len(outs),
        scratch_shapes=scratch,
        cost_estimate=cost,
        compiler_params=pltpu.CompilerParams(vmem_limit_bytes=limit),
    )


def shape_of(shape, dtype):
    return jax.ShapeDtypeStruct(shape, dtype)


def shifted(values, axes, step):
    count = lax.axis_size(axes)
    return lax.ppermute(values, axes, [(i, (i + step) % count) for i in range(count)])


def pack_body(owners, slots, rows, payload, owner_mem, slot_mem, row_mem, tail_mem, sems, out_sems):
    count, depth, width = rows.shape
    lanes = payload.shape[2]
    parts = width // lanes
    loads = [
        pltpu.make_async_copy(owners, owner_mem, sems.at[0]),
        pltpu.make_async_copy(slots, slot_mem, sems.at[1]),
    ]
    loads += [pltpu.make_async_copy(rows.at[j], row_mem.at[j], sems.at[2 + j]) for j in range(count)]
    for load in loads:
        load.start()
    loads[0].wait()
    loads[1].wait()
    copies = []
    for j in range(count):
        mark = jnp.full((SLOT_ROWS, lanes), slot_mem[j].astype(jnp.float32))
        tail_mem[j] = mark.astype(payload.dtype)
        tail = payload.at[owner_mem[j], pl.ds(parts * depth, SLOT_ROWS)]
        copies.append(pltpu.make_async_copy(tail_mem.at[j], tail, out_sems.at[j, parts]))
        copies[-1].start()
    for j in range(count):
        loads[2 + j].wait()
        for part in range(parts):
            block = row_mem.at[j, :, pl.ds(part * lanes, lanes)]
            place = payload.at[owner_mem[j], pl.ds(part * depth, depth)]
            copies.append(pltpu.make_async_copy(block, place, out_sems.at[j, part]))
            copies[-1].start()
    for copy in copies:
        copy.wait()


def pack(rows, owners, slots):
    count, depth, width = rows.shape
    parts = width // LANES
    return call(
        pack_body,
        [shape_of((count, parts * depth + SLOT_ROWS, LANES), rows.dtype)],
        [IN_HBM] * 3,
        scratch=[
            pltpu.SMEM(owners.shape, owners.dtype),
            pltpu.SMEM(slots.shape, slots.dtype),
            pltpu.VMEM(rows.shape, rows.dtype),
            pltpu.VMEM((count, SLOT_ROWS, LANES), rows.dtype),
            pltpu.SemaphoreType.DMA((count + 2,)),
            pltpu.SemaphoreType.DMA((count, parts + 1)),
        ],
        out_spec=IN_HBM,
        limit=PACK_LIMIT,
    )(owners, slots, rows)[0]


def each_core(body):
    core = lax.axis_index("tc")

    @pl.when(core == 0)
    def _():
        body((1, 0))

    @pl.when(core != 0)
    def _():
        body((0, 1))


def logical(listed):
    return [listed[ORDER.index(i)] for i in range(len(ORDER))]


def cut_faces(field, faces):
    faces = logical(faces)

    def cut(order):
        for place, axis in enumerate(order):
            for f in range(4):
                faces[2 * place][f] = field[HIGH[axis][f]]
                faces[2 * place + 1][f] = field[LOW[axis][f]]

    each_core(cut)
    for f in range(4):
        faces[4][f] = field[HIGH[2][f]]
        faces[5][f] = field[LOW[2][f]]


def place_body(landed, field, *faces):
    depth, width = field.shape[1], field.shape[2]
    lanes = landed.shape[2]
    parts = width // lanes
    for j in range(SITES):
        mark = landed[j, parts * depth : parts * depth + SLOT_ROWS, :].astype(jnp.float32)
        slot = jnp.max(mark).astype(jnp.int32)
        for part in range(parts):
            block = landed[j, part * depth : (part + 1) * depth, :]
            field[slot, :, part * lanes : (part + 1) * lanes] = block
    cut_faces(field, faces)


def place(landed, depth, width):
    face = shape_of((4, depth, width), landed.dtype)
    field = shape_of((landed.shape[0], depth, width), landed.dtype)
    out = call(place_body, [field] + [face] * 6, [WHOLE])(landed)
    return out[0], out[1:]


def crossed(values, first, step):
    sizes = [lax.axis_size(axis) for axis in ALL_AXES]
    pairs = []
    for start in np.ndindex(*sizes):
        to = list(start)
        axis = GZ if start[TC] == first else GY
        to[axis] = (to[axis] + step) % sizes[axis]
        pairs.append(tuple(int(np.ravel_multi_index(at, sizes)) for at in (start, to)))
    return lax.ppermute(values, ALL_AXES, pairs)


def exchange(faces):
    faces = logical(faces)
    ahead, behind = crossed(faces[0], 0, 1), crossed(faces[1], 0, -1)
    ahead_b, behind_b = crossed(faces[2], 1, 1), crossed(faces[3], 1, -1)
    before_t = shifted(faces[4], TIME_AXES, 1)
    behind_t = shifted(faces[5], TIME_AXES, -1)
    received = [ahead, behind, ahead_b, behind_b, before_t, behind_t]
    return [received[i] for i in ORDER]


def near_product(s, inside, field):
    own = field[s]
    operand = jnp.concatenate([own, own, own] + [field[s ^ bit] for bit in BITS], axis=0)
    return jnp.dot(inside[s], operand, preferred_element_type=jnp.float32)


def near_body(inside, field, out):
    for s in range(SITES):
        out[s] = near_product(s, inside, field)


def near_cost(field):
    count, depth, width = field.shape
    return pl.CostEstimate(
        flops=2 * count * depth * 6 * depth * width, bytes_accessed=4 * 2**20, transcendentals=0
    )


def near(inside, field):
    return call(near_body, [shape_of(field.shape, jnp.float32)], [WHOLE] * 2, near_cost(field))(
        inside, field
    )[0]


def fold(values):
    return jnp.sum(values.reshape((values.shape[0] // 8, 8, values.shape[1])), axis=0)


def row_sums(sums):
    return jnp.concatenate([jnp.sum(a, axis=0, keepdims=True) for a in sums], axis=0)


def halves(values):
    half = values.shape[0] // 2
    return values[:half], values[half:]


def near_sums_body(inside, field, image, source, out, early):
    sums = [jnp.zeros((8, image.shape[2]), jnp.float32) for _ in range(3)]
    for s in range(SITES):
        out[s] = near_product(s, inside, field)
        i_re, i_im = halves(image[s])
        s_re, s_im = halves(source[s].astype(jnp.float32))
        terms = (
            i_re * i_re + i_im * i_im,
            i_re * s_re + i_im * s_im,
            i_re * s_im - i_im * s_re,
        )
        sums = [a + fold(b) for a, b in zip(sums, terms)]
    early[...] = row_sums(sums + [jnp.zeros((8, image.shape[2]), jnp.float32)] * 5)


def near_sums(inside, field, image, source):
    outs = [shape_of(field.shape, jnp.float32), shape_of((8, field.shape[2]), jnp.float32)]
    return call(near_sums_body, outs, [WHOLE] * 4, near_cost(field))(inside, field, image, source)


def far_operand(s, received, order):
    parts = [None] * 3
    for place, axis in enumerate(order + (2,)):
        if s & BITS[axis]:
            parts[axis] = received[2 * place + 1][HIGH[axis].index(s)]
        else:
            parts[axis] = received[2 * place][LOW[axis].index(s)]
    return jnp.concatenate(parts, axis=0)


def image_body(outside, partial, r0, r1, r2, r3, r4, r5, image, field, *faces):
    received = logical((r0, r1, r2, r3, r4, r5))

    def add(order):
        for s in range(SITES):
            operand = far_operand(s, received, order)
            total = partial[s] + jnp.dot(outside[s], operand, preferred_element_type=jnp.float32)
            image[s] = total
            field[s] = total.astype(field.dtype)

    each_core(add)
    cut_faces(field, faces)


def first_image(outside, partial, received):
    count, depth, width = partial.shape
    dtype = received[0].dtype
    outs = [shape_of(partial.shape, jnp.float32), shape_of(partial.shape, dtype)]
    outs += [shape_of((4, depth, width), dtype)] * 6
    out = call(image_body, outs, [WHOLE] * 8)(outside, partial, *received)
    return out[0], out[1], out[2:]


def sums_body(outside, partial, early, r0, r1, r2, r3, r4, r5, image, source, out):
    received = logical((r0, r1, r2, r3, r4, r5))

    def add(order):
        sums = [jnp.zeros((8, image.shape[2]), jnp.float32) for _ in range(5)]
        for s in range(SITES):
            operand = far_operand(s, received, order)
            second = partial[s] + jnp.dot(outside[s], operand, preferred_element_type=jnp.float32)
            w_re, w_im = halves(second)
            i_re, i_im = halves(image[s])
            s_re, s_im = halves(source[s].astype(jnp.float32))
            terms = (
                i_re * w_re + i_im * w_im,
                i_re * w_im - i_im * w_re,
                w_re * s_re + w_im * s_im,
                w_re * s_im - w_im * s_re,
                w_re * w_re + w_im * w_im,
            )
            sums = [a + fold(b) for a, b in zip(sums, terms)]
        nothing = jnp.zeros((8, image.shape[2]), jnp.float32)
        out[...] = early[...] + row_sums([nothing] * 3 + sums)

    each_core(add)


def local_sums(outside, partial, early, received, image, source):
    return call(sums_body, [shape_of(early.shape, early.dtype)], [WHOLE] * 11)(
        outside, partial, early, *received, image, source
    )[0]


def combine_body(landed, image, source, out, held, sems):
    half = image.shape[1] // 2
    copies = []
    totals = jnp.sum(landed[...], axis=0)
    norm, c_re, c_im, d_re, d_im, e_re, e_im, tail = [totals[i : i + 1] for i in range(8)]
    a_re, a_im = c_re / norm, c_im / norm
    g_re, g_im = d_re / norm, d_im / norm
    p_re, p_im = c_re - a_re * norm, c_im - a_im * norm
    q_re = e_re - (a_re * d_re + a_im * d_im)
    q_im = e_im - (a_im * d_re - a_re * d_im)
    num_re = g_re * p_re + g_im * p_im - q_re
    num_im = g_re * p_im - g_im * p_re - q_im
    denom = tail - (g_re * d_re + g_im * d_im)
    y_re, y_im = num_re / denom, num_im / denom
    x_re = a_re + y_re * g_re - y_im * g_im
    x_im = a_im + y_re * g_im + y_im * g_re
    for s in range(SITES):
        i_re, i_im = halves(image[s])
        s_re, s_im = halves(source[s].astype(jnp.float32))
        out_re = x_re * s_re - x_im * s_im - (y_re * i_re - y_im * i_im)
        out_im = x_re * s_im + x_im * s_re - (y_re * i_im + y_im * i_re)
        held[s, 0:half, :] = out_re.astype(held.dtype)
        held[s, half:, :] = out_im.astype(held.dtype)
        copies.append(pltpu.make_async_copy(held.at[s], out.at[s], sems.at[s]))
        copies[s].start()
    for copy in copies:
        copy.wait()


def combine(landed, image, source):
    return call(
        combine_body,
        [shape_of(source.shape, source.dtype)],
        [WHOLE] * 3,
        scratch=[pltpu.VMEM(source.shape, source.dtype), pltpu.SemaphoreType.DMA((SITES,))],
        out_spec=IN_HBM,
    )(landed, image, source)[0]


def split_body(couplings, inside, outside):
    half, width = couplings.shape[2], couplings.shape[3]
    real_lanes = lax.broadcasted_iota(jnp.int32, (half, width), 1) < width // 2

    def put(target, s, j, k):
        block = couplings[k, s].astype(jnp.float32)
        upper = jnp.where(real_lanes, block, -block)
        lower = pltpu.roll(block, width // 2, 1)
        target[s, 0:half, j * width : (j + 1) * width] = upper.astype(target.dtype)
        target[s, half:, j * width : (j + 1) * width] = lower.astype(target.dtype)

    for s in range(SITES):
        for k in range(3):
            put(inside, s, k, k)
        for axis, bit in enumerate(BITS):
            ahead, behind = 3 + 2 * axis, 4 + 2 * axis
            put(inside, s, 3 + axis, behind if s & bit else ahead)
            put(outside, s, axis, ahead if s & bit else behind)


def split_couplings(couplings):
    blocks = couplings.reshape((couplings.shape[0], SITES) + couplings.shape[-2:])
    width = blocks.shape[-1]
    outs = [shape_of((SITES, width, n * width), blocks.dtype) for n in (6, 3)]
    return call(split_body, outs, [WHOLE])(blocks)


def copies_of(parts, axes):
    return jnp.broadcast_to(parts[None], (lax.axis_size(axes),) + parts.shape)


def everyone(parts, axes):
    return lax.all_to_all(parts, axes, split_axis=0, concat_axis=0, tiled=True)


def local(restricted, couplings, owners, coarse_site):
    count, width = restricted.shape[0], restricted.shape[-1]
    rows = restricted.reshape(count, -1, width)
    landed = everyone(pack(rows, owners, coarse_site), "gz")
    landed, inside, outside = lax.optimization_barrier((landed, *split_couplings(couplings)))
    source, faces = place(landed, rows.shape[1], width)
    received = exchange(faces)
    image, field, faces = first_image(outside, near(inside, source), received)
    received = exchange(faces)
    partial, early = near_sums(inside, field, image, source)
    parts = local_sums(outside, partial, early, received, image, source)
    parts = jnp.sum(lax.all_gather(parts, "tc"), axis=0)
    parts = jnp.sum(everyone(copies_of(parts, ("yb", "gz")), ("yb", "gz")), axis=0)
    parts = everyone(copies_of(parts, ("ya", "gy")), ("ya", "gy"))
    out = combine(parts, image, source)
    return out.reshape(couplings.shape[1:5] + restricted.shape[1:])


def solution(mesh):
    count = mesh.shape["ta"]
    fine = Mesh(mesh.devices.reshape((count // 4, 2, 2) + mesh.devices.shape[1:]), ALL_AXES)
    return jax.shard_map(
        local,
        mesh=fine,
        in_specs=(
            P(ALL_AXES, None, None, None),
            P(None, None, "gy", "gz", TIME_AXES, None, None),
            P(ALL_AXES),
            P(ALL_AXES),
        ),
        out_specs=P(None, "gy", "gz", TIME_AXES, None, None, None),
        check_vma=False,
    )
```

```python
import jax
import jax.numpy as jnp
from jax import lax
from jax.experimental import pallas as pl
from jax.experimental.pallas import tpu as pltpu
import numpy as np
from jax.sharding import Mesh, PartitionSpec as P

ALL_AXES = ("ya", "yb", "tc", "gz", "gy")
TIME_AXES = ("ya", "yb", "tc")
TC, GZ, GY = 2, 3, 4
ORDER = (0, 1, 2, 4, 3, 5)
SLOT_ROWS = 16
LANES = 128
SITES = 8
BITS = (4, 2, 1)
LOW = tuple(tuple(s for s in range(SITES) if not s & bit) for bit in BITS)
HIGH = tuple(tuple(s for s in range(SITES) if s & bit) for bit in BITS)
VMEM_LIMIT = 24 * 1024 * 1024
PACK_LIMIT = 60 * 1024 * 1024
WHOLE = pl.BlockSpec(memory_space=pltpu.VMEM)
IN_HBM = pl.BlockSpec(memory_space=pltpu.HBM)


def call(body, outs, ins, cost=None, scratch=(), out_spec=WHOLE, limit=VMEM_LIMIT):
    return pl.pallas_call(
        body,
        out_shape=outs,
        in_specs=ins,
        out_specs=[out_spec] * len(outs),
        scratch_shapes=scratch,
        cost_estimate=cost,
        compiler_params=pltpu.CompilerParams(vmem_limit_bytes=limit),
    )


def shape_of(shape, dtype):
    return jax.ShapeDtypeStruct(shape, dtype)


def shifted(values, axes, step):
    count = lax.axis_size(axes)
    return lax.ppermute(values, axes, [(i, (i + step) % count) for i in range(count)])


def pack_body(owners, slots, rows, payload, owner_mem, slot_mem, row_mem, tail_mem, sems, out_sems):
    count, depth, width = rows.shape
    lanes = payload.shape[2]
    parts = width // lanes
    loads = [
        pltpu.make_async_copy(owners, owner_mem, sems.at[0]),
        pltpu.make_async_copy(slots, slot_mem, sems.at[1]),
    ]
    loads += [pltpu.make_async_copy(rows.at[j], row_mem.at[j], sems.at[2 + j]) for j in range(count)]
    for load in loads:
        load.start()
    loads[0].wait()
    loads[1].wait()
    copies = []
    for j in range(count):
        mark = jnp.full((SLOT_ROWS, lanes), slot_mem[j].astype(jnp.float32))
        tail_mem[j] = mark.astype(payload.dtype)
        tail = payload.at[owner_mem[j], pl.ds(parts * depth, SLOT_ROWS)]
        copies.append(pltpu.make_async_copy(tail_mem.at[j], tail, out_sems.at[j, parts]))
        copies[-1].start()
    for j in range(count):
        loads[2 + j].wait()
        for part in range(parts):
            block = row_mem.at[j, :, pl.ds(part * lanes, lanes)]
            place = payload.at[owner_mem[j], pl.ds(part * depth, depth)]
            copies.append(pltpu.make_async_copy(block, place, out_sems.at[j, part]))
            copies[-1].start()
    for copy in copies:
        copy.wait()


def pack(rows, owners, slots):
    count, depth, width = rows.shape
    parts = width // LANES
    return call(
        pack_body,
        [shape_of((count, parts * depth + SLOT_ROWS, LANES), rows.dtype)],
        [IN_HBM] * 3,
        scratch=[
            pltpu.SMEM(owners.shape, owners.dtype),
            pltpu.SMEM(slots.shape, slots.dtype),
            pltpu.VMEM(rows.shape, rows.dtype),
            pltpu.VMEM((count, SLOT_ROWS, LANES), rows.dtype),
            pltpu.SemaphoreType.DMA((count + 2,)),
            pltpu.SemaphoreType.DMA((count, parts + 1)),
        ],
        out_spec=IN_HBM,
        limit=PACK_LIMIT,
    )(owners, slots, rows)[0]


def each_core(body):
    core = lax.axis_index("tc")

    @pl.when(core == 0)
    def _():
        body((1, 0))

    @pl.when(core != 0)
    def _():
        body((0, 1))


def logical(listed):
    return [listed[ORDER.index(i)] for i in range(len(ORDER))]


def cut_faces(field, faces):
    faces = logical(faces)

    def cut(order):
        for place, axis in enumerate(order):
            for f in range(4):
                faces[2 * place][f] = field[HIGH[axis][f]]
                faces[2 * place + 1][f] = field[LOW[axis][f]]

    each_core(cut)
    for f in range(4):
        faces[4][f] = field[HIGH[2][f]]
        faces[5][f] = field[LOW[2][f]]


def place_body(landed, field, *faces):
    depth, width = field.shape[1], field.shape[2]
    lanes = landed.shape[2]
    parts = width // lanes
    for j in range(SITES):
        mark = landed[j, parts * depth : parts * depth + SLOT_ROWS, :].astype(jnp.float32)
        slot = jnp.max(mark).astype(jnp.int32)
        for part in range(parts):
            block = landed[j, part * depth : (part + 1) * depth, :]
            field[slot, :, part * lanes : (part + 1) * lanes] = block
    cut_faces(field, faces)


def place(landed, depth, width):
    face = shape_of((4, depth, width), landed.dtype)
    field = shape_of((landed.shape[0], depth, width), landed.dtype)
    out = call(place_body, [field] + [face] * 6, [WHOLE])(landed)
    return out[0], out[1:]


def crossed(values, first, step):
    sizes = [lax.axis_size(axis) for axis in ALL_AXES]
    pairs = []
    for start in np.ndindex(*sizes):
        to = list(start)
        axis = GZ if start[TC] == first else GY
        to[axis] = (to[axis] + step) % sizes[axis]
        pairs.append(tuple(int(np.ravel_multi_index(at, sizes)) for at in (start, to)))
    return lax.ppermute(values, ALL_AXES, pairs)


def exchange(faces):
    faces = logical(faces)
    ahead, behind = crossed(faces[0], 0, 1), crossed(faces[1], 0, -1)
    ahead_b, behind_b = crossed(faces[2], 1, 1), crossed(faces[3], 1, -1)
    before_t = shifted(faces[4], TIME_AXES, 1)
    behind_t = shifted(faces[5], TIME_AXES, -1)
    received = [ahead, behind, ahead_b, behind_b, before_t, behind_t]
    return [received[i] for i in ORDER]


def near_product(s, inside, field):
    own = field[s]
    operand = jnp.concatenate([own, own, own] + [field[s ^ bit] for bit in BITS], axis=0)
    return jnp.dot(inside[s], operand, preferred_element_type=jnp.float32)


def near_body(inside, field, out):
    for s in range(SITES):
        out[s] = near_product(s, inside, field)


def near_cost(field):
    count, depth, width = field.shape
    return pl.CostEstimate(
        flops=2 * count * depth * 6 * depth * width, bytes_accessed=4 * 2**20, transcendentals=0
    )


def near(inside, field):
    return call(near_body, [shape_of(field.shape, jnp.float32)], [WHOLE] * 2, near_cost(field))(
        inside, field
    )[0]


def fold(values):
    return jnp.sum(values.reshape((values.shape[0] // 8, 8, values.shape[1])), axis=0)


def row_sums(sums):
    return jnp.concatenate([jnp.sum(a, axis=0, keepdims=True) for a in sums], axis=0)


def halves(values):
    half = values.shape[0] // 2
    return values[:half], values[half:]


def near_sums_body(inside, field, image, source, out, early):
    sums = [jnp.zeros((8, image.shape[2]), jnp.float32) for _ in range(3)]
    for s in range(SITES):
        out[s] = near_product(s, inside, field)
        i_re, i_im = halves(image[s])
        s_re, s_im = halves(source[s].astype(jnp.float32))
        terms = (
            i_re * i_re + i_im * i_im,
            i_re * s_re + i_im * s_im,
            i_re * s_im - i_im * s_re,
        )
        sums = [a + fold(b) for a, b in zip(sums, terms)]
    early[...] = row_sums(sums + [jnp.zeros((8, image.shape[2]), jnp.float32)] * 5)


def near_sums(inside, field, image, source):
    outs = [shape_of(field.shape, jnp.float32), shape_of((8, field.shape[2]), jnp.float32)]
    return call(near_sums_body, outs, [WHOLE] * 4, near_cost(field))(inside, field, image, source)


def far_products(s, outside, received, order, late):
    total = 0.0
    for place, axis in enumerate(order + (2,)):
        ahead = s & BITS[axis] != 0
        if late == (ahead and place > 0):
            face = received[2 * place + (1 if ahead else 0)]
            block = outside[s, :, axis * face.shape[1] : (axis + 1) * face.shape[1]]
            operand = face[(HIGH if ahead else LOW)[axis].index(s)]
            total = total + jnp.dot(block, operand, preferred_element_type=jnp.float32)
    return total


def early_body(outside, partial, r0, r1, r2, r4, out):
    received = (r0, r1, r2, None, r4, None)

    def add(order):
        for s in range(SITES):
            out[s] = partial[s] + far_products(s, outside, received, order, False)

    each_core(add)


def early_far(outside, partial, received):
    r0, r1, r2, _, r4, _ = logical(received)
    return call(early_body, [shape_of(partial.shape, partial.dtype)], [WHOLE] * 6, near_cost(partial))(
        outside, partial, r0, r1, r2, r4
    )[0]


def image_body(outside, partial, r3, r5, image, field, *faces):
    received = (None, None, None, r3, None, r5)

    def add(order):
        for s in range(SITES):
            total = partial[s] + far_products(s, outside, received, order, True)
            image[s] = total
            field[s] = total.astype(field.dtype)

    each_core(add)
    cut_faces(field, faces)


def first_image(outside, partial, received):
    count, depth, width = partial.shape
    dtype = received[0].dtype
    outs = [shape_of(partial.shape, jnp.float32), shape_of(partial.shape, dtype)]
    outs += [shape_of((4, depth, width), dtype)] * 6
    _, _, _, r3, _, r5 = logical(received)
    out = call(image_body, outs, [WHOLE] * 4)(outside, partial, r3, r5)
    return out[0], out[1], out[2:]


def sums_body(outside, partial, early, r3, r5, image, source, out):
    received = (None, None, None, r3, None, r5)

    def add(order):
        sums = [jnp.zeros((8, image.shape[2]), jnp.float32) for _ in range(5)]
        for s in range(SITES):
            second = partial[s] + far_products(s, outside, received, order, True)
            w_re, w_im = halves(second)
            i_re, i_im = halves(image[s])
            s_re, s_im = halves(source[s].astype(jnp.float32))
            terms = (
                i_re * w_re + i_im * w_im,
                i_re * w_im - i_im * w_re,
                w_re * s_re + w_im * s_im,
                w_re * s_im - w_im * s_re,
                w_re * w_re + w_im * w_im,
            )
            sums = [a + fold(b) for a, b in zip(sums, terms)]
        nothing = jnp.zeros((8, image.shape[2]), jnp.float32)
        out[...] = early[...] + row_sums([nothing] * 3 + sums)

    each_core(add)


def local_sums(outside, partial, early, received, image, source):
    _, _, _, r3, _, r5 = logical(received)
    return call(sums_body, [shape_of(early.shape, early.dtype)], [WHOLE] * 7)(
        outside, partial, early, r3, r5, image, source
    )[0]


def combine_body(landed, image, source, out, held, sems):
    half = image.shape[1] // 2
    copies = []
    totals = jnp.sum(landed[...], axis=0)
    norm, c_re, c_im, d_re, d_im, e_re, e_im, tail = [totals[i : i + 1] for i in range(8)]
    a_re, a_im = c_re / norm, c_im / norm
    g_re, g_im = d_re / norm, d_im / norm
    p_re, p_im = c_re - a_re * norm, c_im - a_im * norm
    q_re = e_re - (a_re * d_re + a_im * d_im)
    q_im = e_im - (a_im * d_re - a_re * d_im)
    num_re = g_re * p_re + g_im * p_im - q_re
    num_im = g_re * p_im - g_im * p_re - q_im
    denom = tail - (g_re * d_re + g_im * d_im)
    y_re, y_im = num_re / denom, num_im / denom
    x_re = a_re + y_re * g_re - y_im * g_im
    x_im = a_im + y_re * g_im + y_im * g_re
    for s in range(SITES):
        i_re, i_im = halves(image[s])
        s_re, s_im = halves(source[s].astype(jnp.float32))
        out_re = x_re * s_re - x_im * s_im - (y_re * i_re - y_im * i_im)
        out_im = x_re * s_im + x_im * s_re - (y_re * i_im + y_im * i_re)
        held[s, 0:half, :] = out_re.astype(held.dtype)
        held[s, half:, :] = out_im.astype(held.dtype)
        copies.append(pltpu.make_async_copy(held.at[s], out.at[s], sems.at[s]))
        copies[s].start()
    for copy in copies:
        copy.wait()


def combine(landed, image, source):
    return call(
        combine_body,
        [shape_of(source.shape, source.dtype)],
        [WHOLE] * 3,
        scratch=[pltpu.VMEM(source.shape, source.dtype), pltpu.SemaphoreType.DMA((SITES,))],
        out_spec=IN_HBM,
    )(landed, image, source)[0]


def split_body(couplings, inside, outside):
    half, width = couplings.shape[2], couplings.shape[3]
    real_lanes = lax.broadcasted_iota(jnp.int32, (half, width), 1) < width // 2

    def put(target, s, j, k):
        block = couplings[k, s].astype(jnp.float32)
        upper = jnp.where(real_lanes, block, -block)
        lower = pltpu.roll(block, width // 2, 1)
        target[s, 0:half, j * width : (j + 1) * width] = upper.astype(target.dtype)
        target[s, half:, j * width : (j + 1) * width] = lower.astype(target.dtype)

    for s in range(SITES):
        for k in range(3):
            put(inside, s, k, k)
        for axis, bit in enumerate(BITS):
            ahead, behind = 3 + 2 * axis, 4 + 2 * axis
            put(inside, s, 3 + axis, behind if s & bit else ahead)
            put(outside, s, axis, ahead if s & bit else behind)


def split_couplings(couplings):
    blocks = couplings.reshape((couplings.shape[0], SITES) + couplings.shape[-2:])
    width = blocks.shape[-1]
    outs = [shape_of((SITES, width, n * width), blocks.dtype) for n in (6, 3)]
    return call(split_body, outs, [WHOLE])(blocks)


def copies_of(parts, axes):
    return jnp.broadcast_to(parts[None], (lax.axis_size(axes),) + parts.shape)


def everyone(parts, axes):
    return lax.all_to_all(parts, axes, split_axis=0, concat_axis=0, tiled=True)


def local(restricted, couplings, owners, coarse_site):
    count, width = restricted.shape[0], restricted.shape[-1]
    rows = restricted.reshape(count, -1, width)
    landed = everyone(pack(rows, owners, coarse_site), "gz")
    landed, inside, outside = lax.optimization_barrier((landed, *split_couplings(couplings)))
    source, faces = place(landed, rows.shape[1], width)
    received = exchange(faces)
    partial = early_far(outside, near(inside, source), received)
    image, field, faces = first_image(outside, partial, received)
    received = exchange(faces)
    partial, early = near_sums(inside, field, image, source)
    partial = early_far(outside, partial, received)
    parts = local_sums(outside, partial, early, received, image, source)
    parts = jnp.sum(lax.all_gather(parts, "tc"), axis=0)
    parts = jnp.sum(everyone(copies_of(parts, ("yb", "gz")), ("yb", "gz")), axis=0)
    parts = everyone(copies_of(parts, ("ya", "gy")), ("ya", "gy"))
    out = combine(parts, image, source)
    return out.reshape(couplings.shape[1:5] + restricted.shape[1:])


def solution(mesh):
    count = mesh.shape["ta"]
    fine = Mesh(mesh.devices.reshape((count // 4, 2, 2) + mesh.devices.shape[1:]), ALL_AXES)
    return jax.shard_map(
        local,
        mesh=fine,
        in_specs=(
            P(ALL_AXES, None, None, None),
            P(None, None, "gy", "gz", TIME_AXES, None, None),
            P(ALL_AXES),
            P(ALL_AXES),
        ),
        out_specs=P(None, "gy", "gz", TIME_AXES, None, None, None),
        check_vma=False,
    )
```

```python
import jax
import jax.numpy as jnp
from jax import lax
from jax.experimental import pallas as pl
from jax.experimental.pallas import tpu as pltpu
import numpy as np
from jax.sharding import Mesh, PartitionSpec as P

ALL_AXES = ("ya", "yb", "tc", "gz", "gy")
TIME_AXES = ("ya", "yb", "tc")
TC, GZ, GY = 2, 3, 4
ORDER = (0, 1, 2, 4, 3, 5)
SLOT_ROWS = 16
LANES = 128
SITES = 8
BITS = (4, 2, 1)
LOW = tuple(tuple(s for s in range(SITES) if not s & bit) for bit in BITS)
HIGH = tuple(tuple(s for s in range(SITES) if s & bit) for bit in BITS)
VMEM_LIMIT = 24 * 1024 * 1024
PACK_LIMIT = 60 * 1024 * 1024
WHOLE = pl.BlockSpec(memory_space=pltpu.VMEM)
IN_HBM = pl.BlockSpec(memory_space=pltpu.HBM)


def call(body, outs, ins, cost=None, scratch=(), out_spec=WHOLE, limit=VMEM_LIMIT):
    return pl.pallas_call(
        body,
        out_shape=outs,
        in_specs=ins,
        out_specs=[out_spec] * len(outs),
        scratch_shapes=scratch,
        cost_estimate=cost,
        compiler_params=pltpu.CompilerParams(vmem_limit_bytes=limit),
    )


def shape_of(shape, dtype):
    return jax.ShapeDtypeStruct(shape, dtype)


def shifted(values, axes, step):
    count = lax.axis_size(axes)
    return lax.ppermute(values, axes, [(i, (i + step) % count) for i in range(count)])


def pack_body(owners, slots, rows, payload, owner_mem, slot_mem, row_mem, tail_mem, sems, out_sems):
    count, depth, width = rows.shape
    lanes = payload.shape[2]
    parts = width // lanes
    loads = [
        pltpu.make_async_copy(owners, owner_mem, sems.at[0]),
        pltpu.make_async_copy(slots, slot_mem, sems.at[1]),
    ]
    loads += [pltpu.make_async_copy(rows.at[j], row_mem.at[j], sems.at[2 + j]) for j in range(count)]
    for load in loads:
        load.start()
    loads[0].wait()
    loads[1].wait()
    copies = []
    for j in range(count):
        mark = jnp.full((SLOT_ROWS, lanes), slot_mem[j].astype(jnp.float32))
        tail_mem[j] = mark.astype(payload.dtype)
        tail = payload.at[owner_mem[j], pl.ds(parts * depth, SLOT_ROWS)]
        copies.append(pltpu.make_async_copy(tail_mem.at[j], tail, out_sems.at[j, parts]))
        copies[-1].start()
    for j in range(count):
        loads[2 + j].wait()
        for part in range(parts):
            block = row_mem.at[j, :, pl.ds(part * lanes, lanes)]
            place = payload.at[owner_mem[j], pl.ds(part * depth, depth)]
            copies.append(pltpu.make_async_copy(block, place, out_sems.at[j, part]))
            copies[-1].start()
    for copy in copies:
        copy.wait()


def pack(rows, owners, slots):
    count, depth, width = rows.shape
    parts = width // LANES
    return call(
        pack_body,
        [shape_of((count, parts * depth + SLOT_ROWS, LANES), rows.dtype)],
        [IN_HBM] * 3,
        scratch=[
            pltpu.SMEM(owners.shape, owners.dtype),
            pltpu.SMEM(slots.shape, slots.dtype),
            pltpu.VMEM(rows.shape, rows.dtype),
            pltpu.VMEM((count, SLOT_ROWS, LANES), rows.dtype),
            pltpu.SemaphoreType.DMA((count + 2,)),
            pltpu.SemaphoreType.DMA((count, parts + 1)),
        ],
        out_spec=IN_HBM,
        limit=PACK_LIMIT,
    )(owners, slots, rows)[0]


def each_core(body):
    core = lax.axis_index("tc")

    @pl.when(core == 0)
    def _():
        body((1, 0))

    @pl.when(core != 0)
    def _():
        body((0, 1))


def logical(listed):
    return [listed[ORDER.index(i)] for i in range(len(ORDER))]


def cut_faces(field, faces):
    faces = logical(faces)

    def cut(order):
        for place, axis in enumerate(order):
            for f in range(4):
                faces[2 * place][f] = field[HIGH[axis][f]]
                faces[2 * place + 1][f] = field[LOW[axis][f]]

    each_core(cut)
    for f in range(4):
        faces[4][f] = field[HIGH[2][f]]
        faces[5][f] = field[LOW[2][f]]


def place_body(landed, field, *faces):
    depth, width = field.shape[1], field.shape[2]
    lanes = landed.shape[2]
    parts = width // lanes
    for j in range(SITES):
        mark = landed[j, parts * depth : parts * depth + SLOT_ROWS, :].astype(jnp.float32)
        slot = jnp.max(mark).astype(jnp.int32)
        for part in range(parts):
            block = landed[j, part * depth : (part + 1) * depth, :]
            field[slot, :, part * lanes : (part + 1) * lanes] = block
    cut_faces(field, faces)


def place(landed, depth, width):
    face = shape_of((4, depth, width), landed.dtype)
    field = shape_of((landed.shape[0], depth, width), landed.dtype)
    out = call(place_body, [field] + [face] * 6, [WHOLE])(landed)
    return out[0], out[1:]


def crossed(values, first, step):
    sizes = [lax.axis_size(axis) for axis in ALL_AXES]
    pairs = []
    for start in np.ndindex(*sizes):
        to = list(start)
        axis = GZ if start[TC] == first else GY
        to[axis] = (to[axis] + step) % sizes[axis]
        pairs.append(tuple(int(np.ravel_multi_index(at, sizes)) for at in (start, to)))
    return lax.ppermute(values, ALL_AXES, pairs)


def exchange(faces):
    faces = logical(faces)
    ahead, behind = crossed(faces[0], 0, 1), crossed(faces[1], 0, -1)
    ahead_b, behind_b = crossed(faces[2], 1, 1), crossed(faces[3], 1, -1)
    before_t = shifted(faces[4], TIME_AXES, 1)
    behind_t = shifted(faces[5], TIME_AXES, -1)
    received = [ahead, behind, ahead_b, behind_b, before_t, behind_t]
    return [received[i] for i in ORDER]


def near_product(s, inside, field):
    own = field[s]
    operand = jnp.concatenate([own, own, own] + [field[s ^ bit] for bit in BITS], axis=0)
    return jnp.dot(inside[s], operand, preferred_element_type=jnp.float32)


def near_body(inside, field, out):
    for s in range(SITES):
        out[s] = near_product(s, inside, field)


def near_cost(field):
    count, depth, width = field.shape
    return pl.CostEstimate(
        flops=2 * count * depth * 6 * depth * width, bytes_accessed=4 * 2**20, transcendentals=0
    )


def near(inside, field):
    return call(near_body, [shape_of(field.shape, jnp.float32)], [WHOLE] * 2, near_cost(field))(
        inside, field
    )[0]


def fold(values):
    return jnp.sum(values.reshape((values.shape[0] // 8, 8, values.shape[1])), axis=0)


def row_sums(sums):
    return jnp.concatenate([jnp.sum(a, axis=0, keepdims=True) for a in sums], axis=0)


def halves(values):
    half = values.shape[0] // 2
    return values[:half], values[half:]


def near_sums_body(inside, field, image, source, out, early):
    sums = [jnp.zeros((8, image.shape[2]), jnp.float32) for _ in range(3)]
    for s in range(SITES):
        out[s] = near_product(s, inside, field)
        i_re, i_im = halves(image[s])
        s_re, s_im = halves(source[s].astype(jnp.float32))
        terms = (
            i_re * i_re + i_im * i_im,
            i_re * s_re + i_im * s_im,
            i_re * s_im - i_im * s_re,
        )
        sums = [a + fold(b) for a, b in zip(sums, terms)]
    early[...] = row_sums(sums + [jnp.zeros((8, image.shape[2]), jnp.float32)] * 5)


def near_sums(inside, field, image, source):
    outs = [shape_of(field.shape, jnp.float32), shape_of((8, field.shape[2]), jnp.float32)]
    return call(near_sums_body, outs, [WHOLE] * 4, near_cost(field))(inside, field, image, source)


def far_operand(s, received, order):
    parts = [None] * 3
    for place, axis in enumerate(order + (2,)):
        if s & BITS[axis]:
            parts[axis] = received[2 * place + 1][HIGH[axis].index(s)]
        else:
            parts[axis] = received[2 * place][LOW[axis].index(s)]
    return jnp.concatenate(parts, axis=0)


def image_body(outside, partial, r0, r1, r2, r3, r4, r5, image, field, *faces):
    received = logical((r0, r1, r2, r3, r4, r5))

    def add(order):
        for s in range(SITES):
            operand = far_operand(s, received, order)
            total = partial[s] + jnp.dot(outside[s], operand, preferred_element_type=jnp.float32)
            image[s] = total
            field[s] = total.astype(field.dtype)

    each_core(add)
    cut_faces(field, faces)


def first_image(outside, partial, received):
    count, depth, width = partial.shape
    dtype = received[0].dtype
    outs = [shape_of(partial.shape, jnp.float32), shape_of(partial.shape, dtype)]
    outs += [shape_of((4, depth, width), dtype)] * 6
    out = call(image_body, outs, [WHOLE] * 8)(outside, partial, *received)
    return out[0], out[1], out[2:]


def sums_body(outside, partial, early, r0, r1, r2, r3, r4, r5, image, source, out):
    received = logical((r0, r1, r2, r3, r4, r5))

    def add(order):
        sums = [jnp.zeros((8, image.shape[2]), jnp.float32) for _ in range(5)]
        for s in range(SITES):
            operand = far_operand(s, received, order)
            second = partial[s] + jnp.dot(outside[s], operand, preferred_element_type=jnp.float32)
            w_re, w_im = halves(second)
            i_re, i_im = halves(image[s])
            s_re, s_im = halves(source[s].astype(jnp.float32))
            terms = (
                i_re * w_re + i_im * w_im,
                i_re * w_im - i_im * w_re,
                w_re * s_re + w_im * s_im,
                w_re * s_im - w_im * s_re,
                w_re * w_re + w_im * w_im,
            )
            sums = [a + fold(b) for a, b in zip(sums, terms)]
        nothing = jnp.zeros((8, image.shape[2]), jnp.float32)
        out[...] = early[...] + row_sums([nothing] * 3 + sums)

    each_core(add)


def local_sums(outside, partial, early, received, image, source):
    return call(sums_body, [shape_of(early.shape, early.dtype)], [WHOLE] * 11)(
        outside, partial, early, *received, image, source
    )[0]


def combine_body(landed, image, source, out, held, sems):
    half = image.shape[1] // 2
    copies = []
    totals = jnp.sum(landed[...], axis=0)
    norm, c_re, c_im, d_re, d_im, e_re, e_im, tail = [totals[i : i + 1] for i in range(8)]
    a_re, a_im = c_re / norm, c_im / norm
    g_re, g_im = d_re / norm, d_im / norm
    p_re, p_im = c_re - a_re * norm, c_im - a_im * norm
    q_re = e_re - (a_re * d_re + a_im * d_im)
    q_im = e_im - (a_im * d_re - a_re * d_im)
    num_re = g_re * p_re + g_im * p_im - q_re
    num_im = g_re * p_im - g_im * p_re - q_im
    denom = tail - (g_re * d_re + g_im * d_im)
    y_re, y_im = num_re / denom, num_im / denom
    x_re = a_re + y_re * g_re - y_im * g_im
    x_im = a_im + y_re * g_im + y_im * g_re
    for s in range(SITES):
        i_re, i_im = halves(image[s])
        s_re, s_im = halves(source[s].astype(jnp.float32))
        out_re = x_re * s_re - x_im * s_im - (y_re * i_re - y_im * i_im)
        out_im = x_re * s_im + x_im * s_re - (y_re * i_im + y_im * i_re)
        held[s, 0:half, :] = out_re.astype(held.dtype)
        held[s, half:, :] = out_im.astype(held.dtype)
        copies.append(pltpu.make_async_copy(held.at[s], out.at[s], sems.at[s]))
        copies[s].start()
    for copy in copies:
        copy.wait()


def combine(landed, image, source):
    return call(
        combine_body,
        [shape_of(source.shape, source.dtype)],
        [WHOLE] * 3,
        scratch=[pltpu.VMEM(source.shape, source.dtype), pltpu.SemaphoreType.DMA((SITES,))],
        out_spec=IN_HBM,
    )(landed, image, source)[0]


def split_body(couplings, inside, outside):
    half, width = couplings.shape[2], couplings.shape[3]
    real_lanes = lax.broadcasted_iota(jnp.int32, (half, width), 1) < width // 2

    def put(target, s, j, k):
        block = couplings[k, s].astype(jnp.float32)
        upper = jnp.where(real_lanes, block, -block)
        lower = pltpu.roll(block, width // 2, 1)
        target[s, 0:half, j * width : (j + 1) * width] = upper.astype(target.dtype)
        target[s, half:, j * width : (j + 1) * width] = lower.astype(target.dtype)

    for s in range(SITES):
        for k in range(3):
            put(inside, s, k, k)
        for axis, bit in enumerate(BITS):
            ahead, behind = 3 + 2 * axis, 4 + 2 * axis
            put(inside, s, 3 + axis, behind if s & bit else ahead)
            put(outside, s, axis, ahead if s & bit else behind)


def split_couplings(couplings):
    blocks = couplings.reshape((couplings.shape[0], SITES) + couplings.shape[-2:])
    width = blocks.shape[-1]
    outs = [shape_of((SITES, width, n * width), blocks.dtype) for n in (6, 3)]
    return call(split_body, outs, [WHOLE])(blocks)


def copies_of(parts, axes):
    return jnp.broadcast_to(parts[None], (lax.axis_size(axes),) + parts.shape)


def everyone(parts, axes):
    return lax.all_to_all(parts, axes, split_axis=0, concat_axis=0, tiled=True)


def local(restricted, couplings, owners, coarse_site):
    count, width = restricted.shape[0], restricted.shape[-1]
    rows = restricted.reshape(count, -1, width)
    landed = everyone(pack(rows, owners, coarse_site), "gz")
    landed, inside, outside = lax.optimization_barrier((landed, *split_couplings(couplings)))
    source, faces = place(landed, rows.shape[1], width)
    received = exchange(faces)
    image, field, faces = first_image(outside, near(inside, source), received)
    received = exchange(faces)
    partial, early = near_sums(inside, field, image, source)
    parts = local_sums(outside, partial, early, received, image, source)
    parts = jnp.sum(everyone(copies_of(parts, ('tc', 'gz')), ('tc', 'gz')), axis=0)
    parts = everyone(copies_of(parts, ('ya', 'yb', 'gy')), ('ya', 'yb', 'gy'))
    out = combine(parts, image, source)
    return out.reshape(couplings.shape[1:5] + restricted.shape[1:])


def solution(mesh):
    count = mesh.shape["ta"]
    fine = Mesh(mesh.devices.reshape((count // 4, 2, 2) + mesh.devices.shape[1:]), ALL_AXES)
    return jax.shard_map(
        local,
        mesh=fine,
        in_specs=(
            P(ALL_AXES, None, None, None),
            P(None, None, "gy", "gz", TIME_AXES, None, None),
            P(ALL_AXES),
            P(ALL_AXES),
        ),
        out_specs=P(None, "gy", "gz", TIME_AXES, None, None, None),
        check_vma=False,
    )
```

```python
import jax
import jax.numpy as jnp
from jax import lax
from jax.experimental import pallas as pl
from jax.experimental.pallas import tpu as pltpu
import numpy as np
from jax.sharding import Mesh, PartitionSpec as P

ALL_AXES = ("ya", "yb", "tc", "gz", "gy")
TIME_AXES = ("ya", "yb", "tc")
TC, GZ, GY = 2, 3, 4
ORDER = (0, 2, 1, 4, 3, 5)
SLOT_ROWS = 16
LANES = 128
SITES = 8
BITS = (4, 2, 1)
LOW = tuple(tuple(s for s in range(SITES) if not s & bit) for bit in BITS)
HIGH = tuple(tuple(s for s in range(SITES) if s & bit) for bit in BITS)
VMEM_LIMIT = 24 * 1024 * 1024
PACK_LIMIT = 60 * 1024 * 1024
WHOLE = pl.BlockSpec(memory_space=pltpu.VMEM)
IN_HBM = pl.BlockSpec(memory_space=pltpu.HBM)


def call(body, outs, ins, cost=None, scratch=(), out_spec=WHOLE, limit=VMEM_LIMIT):
    return pl.pallas_call(
        body,
        out_shape=outs,
        in_specs=ins,
        out_specs=[out_spec] * len(outs),
        scratch_shapes=scratch,
        cost_estimate=cost,
        compiler_params=pltpu.CompilerParams(vmem_limit_bytes=limit),
    )


def shape_of(shape, dtype):
    return jax.ShapeDtypeStruct(shape, dtype)


def shifted(values, axes, step):
    count = lax.axis_size(axes)
    return lax.ppermute(values, axes, [(i, (i + step) % count) for i in range(count)])


def pack_body(owners, slots, rows, payload, owner_mem, slot_mem, row_mem, tail_mem, sems, out_sems):
    count, depth, width = rows.shape
    lanes = payload.shape[2]
    parts = width // lanes
    loads = [
        pltpu.make_async_copy(owners, owner_mem, sems.at[0]),
        pltpu.make_async_copy(slots, slot_mem, sems.at[1]),
    ]
    loads += [pltpu.make_async_copy(rows.at[j], row_mem.at[j], sems.at[2 + j]) for j in range(count)]
    for load in loads:
        load.start()
    loads[0].wait()
    loads[1].wait()
    copies = []
    for j in range(count):
        mark = jnp.full((SLOT_ROWS, lanes), slot_mem[j].astype(jnp.float32))
        tail_mem[j] = mark.astype(payload.dtype)
        tail = payload.at[owner_mem[j], pl.ds(parts * depth, SLOT_ROWS)]
        copies.append(pltpu.make_async_copy(tail_mem.at[j], tail, out_sems.at[j, parts]))
        copies[-1].start()
    for j in range(count):
        loads[2 + j].wait()
        for part in range(parts):
            block = row_mem.at[j, :, pl.ds(part * lanes, lanes)]
            place = payload.at[owner_mem[j], pl.ds(part * depth, depth)]
            copies.append(pltpu.make_async_copy(block, place, out_sems.at[j, part]))
            copies[-1].start()
    for copy in copies:
        copy.wait()


def pack(rows, owners, slots):
    count, depth, width = rows.shape
    parts = width // LANES
    return call(
        pack_body,
        [shape_of((count, parts * depth + SLOT_ROWS, LANES), rows.dtype)],
        [IN_HBM] * 3,
        scratch=[
            pltpu.SMEM(owners.shape, owners.dtype),
            pltpu.SMEM(slots.shape, slots.dtype),
            pltpu.VMEM(rows.shape, rows.dtype),
            pltpu.VMEM((count, SLOT_ROWS, LANES), rows.dtype),
            pltpu.SemaphoreType.DMA((count + 2,)),
            pltpu.SemaphoreType.DMA((count, parts + 1)),
        ],
        out_spec=IN_HBM,
        limit=PACK_LIMIT,
    )(owners, slots, rows)[0]


def each_core(body):
    core = lax.axis_index("tc")

    @pl.when(core == 0)
    def _():
        body((1, 0))

    @pl.when(core != 0)
    def _():
        body((0, 1))


def logical(listed):
    return [listed[ORDER.index(i)] for i in range(len(ORDER))]


def cut_faces(field, faces):
    faces = logical(faces)

    def cut(order):
        for place, axis in enumerate(order):
            for f in range(4):
                faces[2 * place][f] = field[HIGH[axis][f]]
                faces[2 * place + 1][f] = field[LOW[axis][f]]

    each_core(cut)
    for f in range(4):
        faces[4][f] = field[HIGH[2][f]]
        faces[5][f] = field[LOW[2][f]]


def place_body(landed, field, *faces):
    depth, width = field.shape[1], field.shape[2]
    lanes = landed.shape[2]
    parts = width // lanes
    for j in range(SITES):
        mark = landed[j, parts * depth : parts * depth + SLOT_ROWS, :].astype(jnp.float32)
        slot = jnp.max(mark).astype(jnp.int32)
        for part in range(parts):
            block = landed[j, part * depth : (part + 1) * depth, :]
            field[slot, :, part * lanes : (part + 1) * lanes] = block
    cut_faces(field, faces)


def place(landed, depth, width):
    face = shape_of((4, depth, width), landed.dtype)
    field = shape_of((landed.shape[0], depth, width), landed.dtype)
    out = call(place_body, [field] + [face] * 6, [WHOLE])(landed)
    return out[0], out[1:]


def crossed(values, first, step):
    sizes = [lax.axis_size(axis) for axis in ALL_AXES]
    pairs = []
    for start in np.ndindex(*sizes):
        to = list(start)
        axis = GZ if start[TC] == first else GY
        to[axis] = (to[axis] + step) % sizes[axis]
        pairs.append(tuple(int(np.ravel_multi_index(at, sizes)) for at in (start, to)))
    return lax.ppermute(values, ALL_AXES, pairs)


def exchange(faces):
    faces = logical(faces)
    ahead, behind = crossed(faces[0], 0, 1), crossed(faces[1], 0, -1)
    ahead_b, behind_b = crossed(faces[2], 1, 1), crossed(faces[3], 1, -1)
    before_t = shifted(faces[4], TIME_AXES, 1)
    behind_t = shifted(faces[5], TIME_AXES, -1)
    received = [ahead, behind, ahead_b, behind_b, before_t, behind_t]
    return [received[i] for i in ORDER]


def near_product(s, inside, field):
    own = field[s]
    operand = jnp.concatenate([own, own, own] + [field[s ^ bit] for bit in BITS], axis=0)
    return jnp.dot(inside[s], operand, preferred_element_type=jnp.float32)


def near_body(inside, field, out):
    for s in range(SITES):
        out[s] = near_product(s, inside, field)


def near_cost(field):
    count, depth, width = field.shape
    return pl.CostEstimate(
        flops=2 * count * depth * 6 * depth * width, bytes_accessed=4 * 2**20, transcendentals=0
    )


def near(inside, field):
    return call(near_body, [shape_of(field.shape, jnp.float32)], [WHOLE] * 2, near_cost(field))(
        inside, field
    )[0]


def fold(values):
    return jnp.sum(values.reshape((values.shape[0] // 8, 8, values.shape[1])), axis=0)


def row_sums(sums):
    return jnp.concatenate([jnp.sum(a, axis=0, keepdims=True) for a in sums], axis=0)


def halves(values):
    half = values.shape[0] // 2
    return values[:half], values[half:]


def near_sums_body(inside, field, image, source, out, early):
    sums = [jnp.zeros((8, image.shape[2]), jnp.float32) for _ in range(3)]
    for s in range(SITES):
        out[s] = near_product(s, inside, field)
        i_re, i_im = halves(image[s])
        s_re, s_im = halves(source[s].astype(jnp.float32))
        terms = (
            i_re * i_re + i_im * i_im,
            i_re * s_re + i_im * s_im,
            i_re * s_im - i_im * s_re,
        )
        sums = [a + fold(b) for a, b in zip(sums, terms)]
    early[...] = row_sums(sums + [jnp.zeros((8, image.shape[2]), jnp.float32)] * 5)


def near_sums(inside, field, image, source):
    outs = [shape_of(field.shape, jnp.float32), shape_of((8, field.shape[2]), jnp.float32)]
    return call(near_sums_body, outs, [WHOLE] * 4, near_cost(field))(inside, field, image, source)


def far_operand(s, received, order):
    parts = [None] * 3
    for place, axis in enumerate(order + (2,)):
        if s & BITS[axis]:
            parts[axis] = received[2 * place + 1][HIGH[axis].index(s)]
        else:
            parts[axis] = received[2 * place][LOW[axis].index(s)]
    return jnp.concatenate(parts, axis=0)


def image_body(outside, partial, r0, r1, r2, r3, r4, r5, image, field, *faces):
    received = logical((r0, r1, r2, r3, r4, r5))

    def add(order):
        for s in range(SITES):
            operand = far_operand(s, received, order)
            total = partial[s] + jnp.dot(outside[s], operand, preferred_element_type=jnp.float32)
            image[s] = total
            field[s] = total.astype(field.dtype)

    each_core(add)
    cut_faces(field, faces)


def first_image(outside, partial, received):
    count, depth, width = partial.shape
    dtype = received[0].dtype
    outs = [shape_of(partial.shape, jnp.float32), shape_of(partial.shape, dtype)]
    outs += [shape_of((4, depth, width), dtype)] * 6
    out = call(image_body, outs, [WHOLE] * 8)(outside, partial, *received)
    return out[0], out[1], out[2:]


def sums_body(outside, partial, early, r0, r1, r2, r3, r4, r5, image, source, out):
    received = logical((r0, r1, r2, r3, r4, r5))

    def add(order):
        sums = [jnp.zeros((8, image.shape[2]), jnp.float32) for _ in range(5)]
        for s in range(SITES):
            operand = far_operand(s, received, order)
            second = partial[s] + jnp.dot(outside[s], operand, preferred_element_type=jnp.float32)
            w_re, w_im = halves(second)
            i_re, i_im = halves(image[s])
            s_re, s_im = halves(source[s].astype(jnp.float32))
            terms = (
                i_re * w_re + i_im * w_im,
                i_re * w_im - i_im * w_re,
                w_re * s_re + w_im * s_im,
                w_re * s_im - w_im * s_re,
                w_re * w_re + w_im * w_im,
            )
            sums = [a + fold(b) for a, b in zip(sums, terms)]
        nothing = jnp.zeros((8, image.shape[2]), jnp.float32)
        out[...] = early[...] + row_sums([nothing] * 3 + sums)

    each_core(add)


def local_sums(outside, partial, early, received, image, source):
    return call(sums_body, [shape_of(early.shape, early.dtype)], [WHOLE] * 11)(
        outside, partial, early, *received, image, source
    )[0]


def combine_body(landed, image, source, out, held, sems):
    half = image.shape[1] // 2
    copies = []
    totals = jnp.sum(landed[...], axis=0)
    norm, c_re, c_im, d_re, d_im, e_re, e_im, tail = [totals[i : i + 1] for i in range(8)]
    a_re, a_im = c_re / norm, c_im / norm
    g_re, g_im = d_re / norm, d_im / norm
    p_re, p_im = c_re - a_re * norm, c_im - a_im * norm
    q_re = e_re - (a_re * d_re + a_im * d_im)
    q_im = e_im - (a_im * d_re - a_re * d_im)
    num_re = g_re * p_re + g_im * p_im - q_re
    num_im = g_re * p_im - g_im * p_re - q_im
    denom = tail - (g_re * d_re + g_im * d_im)
    y_re, y_im = num_re / denom, num_im / denom
    x_re = a_re + y_re * g_re - y_im * g_im
    x_im = a_im + y_re * g_im + y_im * g_re
    for s in range(SITES):
        i_re, i_im = halves(image[s])
        s_re, s_im = halves(source[s].astype(jnp.float32))
        out_re = x_re * s_re - x_im * s_im - (y_re * i_re - y_im * i_im)
        out_im = x_re * s_im + x_im * s_re - (y_re * i_im + y_im * i_re)
        held[s, 0:half, :] = out_re.astype(held.dtype)
        held[s, half:, :] = out_im.astype(held.dtype)
        copies.append(pltpu.make_async_copy(held.at[s], out.at[s], sems.at[s]))
        copies[s].start()
    for copy in copies:
        copy.wait()


def combine(landed, image, source):
    return call(
        combine_body,
        [shape_of(source.shape, source.dtype)],
        [WHOLE] * 3,
        scratch=[pltpu.VMEM(source.shape, source.dtype), pltpu.SemaphoreType.DMA((SITES,))],
        out_spec=IN_HBM,
    )(landed, image, source)[0]


def split_body(couplings, inside, outside):
    half, width = couplings.shape[2], couplings.shape[3]
    real_lanes = lax.broadcasted_iota(jnp.int32, (half, width), 1) < width // 2

    def put(target, s, j, k):
        block = couplings[k, s].astype(jnp.float32)
        upper = jnp.where(real_lanes, block, -block)
        lower = pltpu.roll(block, width // 2, 1)
        target[s, 0:half, j * width : (j + 1) * width] = upper.astype(target.dtype)
        target[s, half:, j * width : (j + 1) * width] = lower.astype(target.dtype)

    for s in range(SITES):
        for k in range(3):
            put(inside, s, k, k)
        for axis, bit in enumerate(BITS):
            ahead, behind = 3 + 2 * axis, 4 + 2 * axis
            put(inside, s, 3 + axis, behind if s & bit else ahead)
            put(outside, s, axis, ahead if s & bit else behind)


def split_couplings(couplings):
    blocks = couplings.reshape((couplings.shape[0], SITES) + couplings.shape[-2:])
    width = blocks.shape[-1]
    outs = [shape_of((SITES, width, n * width), blocks.dtype) for n in (6, 3)]
    return call(split_body, outs, [WHOLE])(blocks)


def copies_of(parts, axes):
    return jnp.broadcast_to(parts[None], (lax.axis_size(axes),) + parts.shape)


def everyone(parts, axes):
    return lax.all_to_all(parts, axes, split_axis=0, concat_axis=0, tiled=True)


def local(restricted, couplings, owners, coarse_site):
    count, width = restricted.shape[0], restricted.shape[-1]
    rows = restricted.reshape(count, -1, width)
    landed = everyone(pack(rows, owners, coarse_site), "gz")
    landed, inside, outside = lax.optimization_barrier((landed, *split_couplings(couplings)))
    source, faces = place(landed, rows.shape[1], width)
    received = exchange(faces)
    image, field, faces = first_image(outside, near(inside, source), received)
    received = exchange(faces)
    partial, early = near_sums(inside, field, image, source)
    parts = local_sums(outside, partial, early, received, image, source)
    parts = jnp.sum(lax.all_gather(parts, "tc"), axis=0)
    parts = jnp.sum(everyone(copies_of(parts, ("yb", "gz")), ("yb", "gz")), axis=0)
    parts = everyone(copies_of(parts, ("ya", "gy")), ("ya", "gy"))
    out = combine(parts, image, source)
    return out.reshape(couplings.shape[1:5] + restricted.shape[1:])


def solution(mesh):
    count = mesh.shape["ta"]
    fine = Mesh(mesh.devices.reshape((count // 4, 2, 2) + mesh.devices.shape[1:]), ALL_AXES)
    return jax.shard_map(
        local,
        mesh=fine,
        in_specs=(
            P(ALL_AXES, None, None, None),
            P(None, None, "gy", "gz", TIME_AXES, None, None),
            P(ALL_AXES),
            P(ALL_AXES),
        ),
        out_specs=P(None, "gy", "gz", TIME_AXES, None, None, None),
        check_vma=False,
    )
```
